32 devices in a mesh: replica: 8 (over z, x), shard: 4 (over y, core).
Axes of the slice: x: 2, y: 2, z: 4, core: 2. Of those that a mesh axis runs over, the one named last changes fastest.
Arguments:
- tokens: bfloat16 [4096, 768], P(('replica', 'shard')), may hold values from -6 to 6
- cotangent: bfloat16 [4096, 768], P(('replica', 'shard')), may hold values from -6 to 6
- seq_lengths: int32 [32, 4], P(('replica', 'shard')), may hold values from 1 to 96, 128 in all within a row
- w_in: bfloat16 [768, 3352], P('shard'), may hold values from -0.21875 to 0.21875
- w_out: bfloat16 [1536, 768], P('shard'), may hold values from -0.15625 to 0.15625
- w_small: bfloat16 [11336], P('shard')
- m_in: float32 [768, 3352], P('shard'), may hold values from -6 to 6
- v_in: float32 [768, 3352], P('shard'), may hold values from 18.432 to 73.728
- m_out: float32 [1536, 768], P('shard'), may hold values from -28 to 28
- v_out: float32 [1536, 768], P('shard'), may hold values from 102.4 to 409.6
- m_small: float32 [11336], P('shard'), may hold values from -20 to 20
- v_small: float32 [11336], P('shard'), may hold values from 51.2 to 204.8
Outputs:
- block_out: bfloat16 [4096, 768], P(('replica', 'shard'))
- grad_tokens: bfloat16 [4096, 768], P(('replica', 'shard'))
- new_w_in: float32 [768, 3352], P('shard')
- new_m_in: float32 [768, 3352], P('shard')
- new_v_in: float32 [768, 3352], P('shard')
- new_w_out: float32 [1536, 768], P('shard')
- new_m_out: float32 [1536, 768], P('shard')
- new_v_out: float32 [1536, 768], P('shard')
- new_w_small: float32 [11336], P('shard')
- new_m_small: float32 [11336], P('shard')
- new_v_small: float32 [11336], P('shard')
The draws below stay inside these ranges and needn't reach their ends.
Inputs may be any that keep to these rules, and one draw needn't show every extreme that they name: `seq_lengths`: in each row the first 3 entries are sequence lengths and the last is the padding at the block's end; each row sums to 128 and its largest entry is 96.
All inputs are finite; a program needn't handle non-finite values.
Results may differ from the reference program's by a relative error of at most 0.0094.
Values may be sent and summed in bfloat16 or wider, within the bound.
A program may use at most 128 MiB of HBM per device.

```python
import math
import jax
import jax.numpy as jnp
import numpy as np
from jax import lax

D = 768
STATE = 128
HEAD = 64
KCONV = 4
SLOTS = 4
STEP = 10
BLOCK = 128
DI = 1536
CIN = 3352
SMALLP = 11336
MOSTLEN = 96
BLOCKS = 32
TOKENS = 4096


def draw_w_small(key, part):
    key = jax.random.fold_in(key, 7)
    channels = DI + 2 * STATE
    heads = DI // HEAD
    keys = jax.random.split(key, 7)
    taps = 0.5 * jax.random.normal(keys[0], (KCONV * channels,), jnp.float32)
    biases = 0.3 * jax.random.normal(keys[1], (channels,), jnp.float32)
    step_init = jnp.exp(jax.random.uniform(keys[2], (heads,), jnp.float32, jnp.log(0.005), jnp.log(0.1)))
    step_bias = jnp.log(jnp.expm1(step_init))
    decay_log = jnp.log(jax.random.uniform(keys[3], (heads,), jnp.float32, 1.0, 16.0))
    skip_gain = jax.random.uniform(keys[4], (heads,), jnp.float32, 0.5, 1.5)
    pre_gain = jax.random.uniform(keys[5], (D,), jnp.float32, 0.6, 1.4)
    gate_gain = jax.random.uniform(keys[6], (DI,), jnp.float32, 0.6, 1.4)
    packed = jnp.concatenate([taps, biases, step_bias, decay_log, skip_gain, pre_gain, gate_gain])
    return packed.astype(jnp.bfloat16)


def levels(rng, shape, shards, low, top_value):
    loudness, own = 1.0, jax.random.fold_in(rng, 6)
    for dim, blocks in shards:
        steps = jnp.exp(jax.random.uniform(jax.random.fold_in(own, dim), (blocks,), jnp.float32, low / len(shards), top_value / len(shards)))
        loudness = loudness * jnp.repeat(steps, shape[dim] // blocks).reshape([-1 if axis == dim else 1 for axis in range(len(shape))])
    return loudness


def split_up(amount, total, limit, slope):
    weights = [(1 << 20) // math.isqrt(rank ** slope) + 1 for rank in range(2, amount + 1)]
    spare, counts = total - limit - (amount - 1), [1] * (amount - 1)
    while spare > 0:
        movable = [i for i in range(amount - 1) if counts[i] < limit]
        mass, left = sum([weights[i] for i in movable]), spare
        for i in movable:
            addition = min(limit - counts[i], max(1, left * weights[i] // mass), spare)
            counts[i] = counts[i] + addition
            spare = spare - addition
    return np.array([limit] + counts)


def ragged_sizes(own_key, amount, total, bound, skew):
    if amount == 2:
        one = jax.random.randint(own_key, (), max(1, total - bound), min(bound, total - 1) + 1)
        return jnp.stack([one, total - one])
    lengths = jnp.asarray(split_up(amount, total, bound, skew), jnp.int32)
    couples = (amount - 1) // 2
    source_of, receiver = lengths[1:1 + 2 * couples:2], lengths[2:2 + 2 * couples:2]
    slack = jnp.minimum(source_of - 1, bound - receiver)
    moved = jax.random.randint(jax.random.fold_in(own_key, 1), (couples,), 0, 1 << 20) % (slack + 1)
    lengths = lengths.at[1:1 + 2 * couples:2].set(source_of - moved).at[2:2 + 2 * couples:2].set(receiver + moved)
    return lengths[jax.random.permutation(jax.random.fold_in(own_key, 2), amount)]


def scatter_about(rng, dims, width, bound, cuts=(), held_as=jnp.bfloat16):
    gain = levels(rng, dims, cuts, -0.22, 0.18) if cuts else 1.0
    entries = jax.random.normal(rng, dims, jnp.float32) * width * gain
    return jnp.minimum(jnp.maximum(entries, -bound), bound).astype(held_as)


def setup_inputs(seed: int = 0) -> dict:
    splits = jax.random.split(jax.random.key(seed), 13)
    return {
        "tokens": scatter_about(splits[0], (TOKENS, D), 1.0, 6.0, ((0, 32),)),
        "cotangent": scatter_about(splits[1], (TOKENS, D), 1.0, 6.0, ((0, 32),)),
        "seq_lengths": jax.vmap(lambda own: ragged_sizes(own, SLOTS, BLOCK, MOSTLEN, 0))(jax.random.split(splits[2], BLOCKS)).reshape((BLOCKS, SLOTS)).astype(jnp.int32),
        "w_in": scatter_about(splits[3], (D, CIN), D ** -0.5, 0.21875, ((0, 4),)),
        "w_out": scatter_about(splits[4], (DI, D), DI ** -0.5, 0.15625, ((0, 4),)),
        "w_small": draw_w_small(jax.random.fold_in(splits[12], 71), 0),
        "m_in": scatter_about(splits[6], (D, CIN), (0.03 * TOKENS ** 0.5), 6.0, ((0, 4),), jnp.float32),
        "v_in": jnp.clip(jnp.exp(math.log(73.728) - 1.3862944 * jax.random.uniform(splits[7], (D, CIN), jnp.float32) ** levels(splits[7], (D, CIN), ((0, 4),), -0.2, 0.2)), 18.432, 73.728),
        "m_out": scatter_about(splits[8], (DI, D), (0.07 * TOKENS ** 0.5), 28.0, ((0, 4),), jnp.float32),
        "v_out": jnp.clip(jnp.exp(math.log(409.6) - 1.3862944 * jax.random.uniform(splits[9], (DI, D), jnp.float32) ** levels(splits[9], (DI, D), ((0, 4),), -0.2, 0.2)), 102.4, 409.6),
        "m_small": scatter_about(splits[10], (SMALLP,), (0.05 * TOKENS ** 0.5), 20.0, ((0, 4),), jnp.float32),
        "v_small": jnp.clip(jnp.exp(math.log(204.8) - 1.3862944 * jax.random.uniform(splits[11], (SMALLP,), jnp.float32) ** levels(splits[11], (SMALLP,), ((0, 4),), -0.2, 0.2)), 51.2, 204.8),
    }


@jax.custom_vjp
def low(v):
    return lax.optimization_barrier(v.astype(jnp.bfloat16)).astype(jnp.float32)

@jax.custom_vjp
def low_back(v):
    return v

def low_keep(v):
    return (low(v), None)

def low_pass(kept, grad):
    return (grad,)

def back_keep(v):
    return (v, None)

def back_low(kept, grad):
    return (low(grad),)
low.defvjp(low_keep, low_pass)
low_back.defvjp(back_keep, back_low)
epsilon = 1e-05
beta_one = 0.9
beta_two = 0.95
adam_eps = 1e-08

def mixer(resid, weight_in, weight_out, packed, seglens, precision_mode):
    rows_count = resid.shape[0]
    channels = DI + 2 * STATE
    heads = DI // HEAD
    kernel = packed[:KCONV * channels].reshape(KCONV, channels)
    conv_bias = packed[KCONV * channels:(KCONV + 1) * channels]
    start = (KCONV + 1) * channels
    step_bias = packed[start:start + heads]
    decay_log = packed[start + heads:start + 2 * heads]
    skip_gain = packed[start + 2 * heads:start + 3 * heads]
    pre_gain = packed[start + 3 * heads:start + 3 * heads + D]
    gate_gain = packed[start + 3 * heads + D:]
    places = jnp.arange(rows_count, dtype=jnp.int32)
    bounds = jnp.cumsum(seglens).astype(jnp.int32)
    segment = lax.optimization_barrier(jnp.sum((places[:, None] >= bounds[None, :]).astype(jnp.int32), axis=1))
    meansq = lax.optimization_barrier(jnp.mean(resid * resid, axis=1, keepdims=True))
    normed = resid * lax.rsqrt(meansq + epsilon) * pre_gain
    project = low_back(jnp.dot(low(normed), weight_in, precision=precision_mode, preferred_element_type=jnp.float32))
    gate_raw = project[:, :DI]
    conv_in = project[:, DI:DI + channels]
    step_raw = project[:, DI + channels:]
    convolved = conv_bias + kernel[KCONV - 1] * conv_in
    for offset in range(1, KCONV):
        shifted = jnp.concatenate([jnp.zeros((offset, channels), jnp.float32), conv_in[:-offset]], axis=0)
        earlier = jnp.concatenate([jnp.full((offset,), -1, jnp.int32), segment[:-offset]])
        within = (earlier == segment).astype(jnp.float32)[:, None]
        convolved = convolved + kernel[KCONV - 1 - offset] * shifted * within
    activated = jax.nn.silu(convolved)
    inner = low(activated[:, :DI])
    in_state = low(activated[:, DI:DI + STATE])
    out_state = low(activated[:, DI + STATE:])
    step_size = jax.nn.softplus(step_raw + step_bias)
    logrates = jnp.cumsum(step_size * -jnp.exp(decay_log), axis=0)
    intersection = low_back(jnp.dot(out_state, in_state.T, precision=precision_mode, preferred_element_type=jnp.float32))
    allowed = (segment[:, None] == segment[None, :]) & (places[:, None] >= places[None, :])
    group_count = heads // 8
    rates_grouped = logrates.reshape(rows_count, group_count, 8).transpose(1, 0, 2)
    steps_grouped = step_size.reshape(rows_count, group_count, 8).transpose(1, 0, 2)
    inner_grouped = inner.reshape(rows_count, group_count, 8, HEAD).transpose(1, 0, 2, 3)

    def mix_group(item):
        rate_part, step_part, inner_part = item
        spread = rate_part.T[:, :, None] - rate_part.T[:, None, :]
        weights = low(intersection[None] * jnp.exp(jnp.where(allowed[None], spread, -1e+30)) * step_part.T[:, None, :])
        return jnp.einsum('hts,shp->thp', weights, inner_part, precision=precision_mode, preferred_element_type=jnp.float32)
    mixed = lax.map(jax.checkpoint(mix_group), (rates_grouped, steps_grouped, inner_grouped))
    scanned = low_back(mixed.transpose(1, 0, 2, 3).reshape(rows_count, DI)) + inner * jnp.repeat(skip_gain, HEAD)
    gated = scanned * jax.nn.silu(gate_raw)
    gatesq = lax.optimization_barrier(jnp.mean(gated * gated, axis=1, keepdims=True))
    normed_two = gated * lax.rsqrt(gatesq + epsilon) * gate_gain
    output = low_back(jnp.dot(low(normed_two), weight_out, precision=precision_mode, preferred_element_type=jnp.float32))
    return resid + output

def adamw(weight, grad, first, second, rate, decay):
    first_new = beta_one * first + (1.0 - beta_one) * grad
    second_new = beta_two * second + (1.0 - beta_two) * grad * grad
    corrected = first_new / (1.0 - beta_one ** STEP) / (jnp.sqrt(second_new / (1.0 - beta_two ** STEP)) + adam_eps)
    master = weight.astype(jnp.float32)
    return (master - rate * (corrected + decay * master), first_new, second_new)

def reference(tokens, cotangent, seq_lengths, w_in, w_out, w_small, m_in, v_in, m_out, v_out, m_small, v_small):
    full_in = w_in.astype(jnp.float32)
    full_out = w_out.astype(jnp.float32)
    full_small = w_small.astype(jnp.float32)
    batched = tokens.astype(jnp.float32).reshape(BLOCKS // 4, 4, BLOCK, D)
    cots = cotangent.astype(jnp.float32).reshape(BLOCKS // 4, 4, BLOCK, D)
    lens = seq_lengths.reshape(BLOCKS // 4, 4, SLOTS)
    places = jnp.arange(BLOCK, dtype=jnp.int32)
    highest = lax.Precision.HIGHEST

    def scan_step(carry, item):
        resid, back, seglens = item

        def forward(resid_in, weight_in, weight_out, packed):
            return jax.vmap(lambda row, lrow: mixer(row, weight_in, weight_out, packed, lrow, highest))(resid_in, seglens)
        result, pullback = jax.vjp(forward, resid, full_in, full_out, full_small)
        valid = (places[None, :] < (BLOCK - seglens[:, -1])[:, None]).astype(jnp.float32)
        grad_x, grad_a, grad_b, grad_c = pullback(back * valid[:, :, None])
        carry = (carry[0] + grad_a, carry[1] + grad_b, carry[2] + grad_c)
        return (carry, (result.astype(jnp.bfloat16), grad_x.astype(jnp.bfloat16)))
    start = (jnp.zeros((D, CIN), jnp.float32), jnp.zeros((DI, D), jnp.float32), jnp.zeros((SMALLP,), jnp.float32))
    totals, outs = lax.scan(scan_step, start, (batched, cots, lens))
    block_out = outs[0].reshape(TOKENS, D)
    grad_tokens = outs[1].reshape(TOKENS, D)
    new_w_in, new_m_in, new_v_in = adamw(w_in, totals[0], m_in, v_in, 0.05, 0.1)
    new_w_out, new_m_out, new_v_out = adamw(w_out, totals[1], m_out, v_out, 0.04, 0.1)
    new_w_small, new_m_small, new_v_small = adamw(w_small, totals[2], m_small, v_small, 0.3, 0.0)
    return (block_out, grad_tokens, new_w_in, new_m_in, new_v_in, new_w_out, new_m_out, new_v_out, new_w_small, new_m_small, new_v_small)
```

```python
import jax
import jax.numpy as jnp
from jax import lax
from jax.experimental import pallas as pl
from jax.experimental.pallas import tpu as pltpu
from jax.sharding import PartitionSpec as P

D = 768
STATE = 128
HEAD = 64
KCONV = 4
STEP = 10
DI = 1536


epsilon = 1e-05
beta_one = 0.9
beta_two = 0.95
adam_eps = 1e-08


def make_rounders():

    def round_plain(value):
        return lax.optimization_barrier(value.astype(jnp.bfloat16)).astype(jnp.float32)

    def unchanged(value):
        return value

    round_value = jax.custom_vjp(round_plain)
    round_grad = jax.custom_vjp(unchanged)

    def value_keep(value):
        return (round_plain(value), None)

    def value_pass(kept, gradient):
        return (gradient,)

    def grad_keep(value):
        return (value, None)

    def grad_round(kept, gradient):
        return (round_plain(gradient),)

    round_value.defvjp(value_keep, value_pass)
    round_grad.defvjp(grad_keep, grad_round)
    return (round_value, round_grad)


def mixer(resid, weight_in, weight_out, packed, seglens, round_value, round_grad):
    rows_count = resid.shape[0]
    channels = DI + 2 * STATE
    heads = DI // HEAD
    kernel = packed[: KCONV * channels].reshape(KCONV, channels)
    conv_bias = packed[KCONV * channels : (KCONV + 1) * channels]
    start = (KCONV + 1) * channels
    step_bias = packed[start : start + heads]
    decay_log = packed[start + heads : start + 2 * heads]
    skip_gain = packed[start + 2 * heads : start + 3 * heads]
    pre_gain = packed[start + 3 * heads : start + 3 * heads + D]
    gate_gain = packed[start + 3 * heads + D :]
    places = jnp.arange(rows_count, dtype=jnp.int32)
    bounds = jnp.cumsum(seglens)
    segment = jnp.sum((places[:, None] >= bounds[None, :]).astype(jnp.int32), axis=1)
    meansq = jnp.mean(resid * resid, axis=1, keepdims=True)
    normed = resid * lax.rsqrt(meansq + epsilon) * pre_gain
    project = round_grad(
        jnp.dot(round_value(normed), weight_in, preferred_element_type=jnp.float32)
    )
    gate_raw = project[:, :DI]
    conv_in = project[:, DI : DI + channels]
    step_raw = project[:, DI + channels :]
    convolved = conv_bias + kernel[KCONV - 1] * conv_in
    for offset in range(1, KCONV):
        shifted = jnp.concatenate(
            [jnp.zeros((offset, channels), jnp.float32), conv_in[:-offset]], axis=0
        )
        earlier = jnp.concatenate([jnp.full((offset,), -1, jnp.int32), segment[:-offset]])
        within = (earlier == segment).astype(jnp.float32)[:, None]
        convolved = convolved + kernel[KCONV - 1 - offset] * shifted * within
    activated = jax.nn.silu(convolved)
    inner = round_value(activated[:, :DI])
    in_state = round_value(activated[:, DI : DI + STATE])
    out_state = round_value(activated[:, DI + STATE :])
    step_size = jax.nn.softplus(step_raw + step_bias)
    logrates = jnp.cumsum(step_size * -jnp.exp(decay_log), axis=0)
    intersection = round_grad(jnp.dot(out_state, in_state.T, preferred_element_type=jnp.float32))
    allowed = (segment[:, None] == segment[None, :]) & (places[:, None] >= places[None, :])
    group_count = heads // 8
    rates_grouped = logrates.reshape(rows_count, group_count, 8).transpose(1, 0, 2)
    steps_grouped = step_size.reshape(rows_count, group_count, 8).transpose(1, 0, 2)
    inner_grouped = inner.reshape(rows_count, group_count, 8, HEAD).transpose(1, 0, 2, 3)

    def mix_group(entry):
        rate_part, step_part, inner_part = entry
        spread = rate_part.T[:, :, None] - rate_part.T[:, None, :]
        weights = round_value(
            intersection[None]
            * jnp.exp(jnp.where(allowed[None], spread, -1e30))
            * step_part.T[:, None, :]
        )
        return jnp.einsum("hts,shp->thp", weights, inner_part, preferred_element_type=jnp.float32)

    mixed = lax.map(jax.checkpoint(mix_group), (rates_grouped, steps_grouped, inner_grouped))
    scanned = round_grad(mixed.transpose(1, 0, 2, 3).reshape(rows_count, DI)) + inner * jnp.repeat(
        skip_gain, HEAD
    )
    gated = scanned * jax.nn.silu(gate_raw)
    gatesq = jnp.mean(gated * gated, axis=1, keepdims=True)
    normed_two = gated * lax.rsqrt(gatesq + epsilon) * gate_gain
    output = round_grad(
        jnp.dot(round_value(normed_two), weight_out, preferred_element_type=jnp.float32)
    )
    return resid + output


def adamw(weight, gradient, first, second, rate, decay):
    first_new = beta_one * first + (1.0 - beta_one) * gradient
    second_new = beta_two * second + (1.0 - beta_two) * gradient * gradient
    corrected = (
        first_new
        / (1.0 - beta_one**STEP)
        / (jnp.sqrt(second_new / (1.0 - beta_two**STEP)) + adam_eps)
    )
    master = weight.astype(jnp.float32)
    return (master - rate * (corrected + decay * master), first_new, second_new)


def reduce_group(grads):
    shares = (
        lax.psum_scatter(grads[0], "shard", scatter_dimension=0, tiled=True),
        lax.psum_scatter(grads[1], "shard", scatter_dimension=0, tiled=True),
        lax.psum_scatter(grads[2], "shard", scatter_dimension=0, tiled=True),
    )
    return lax.psum((shares[0], shares[1], shares[2]), "replica")


def on_device(
    tokens, cotangent, seq_lengths, w_in, w_out, w_small, m_in, v_in, m_out, v_out, m_small, v_small
):
    round_value, round_grad = make_rounders()
    full_in, full_out, full_small = (
        lax.all_gather(w_in, "shard", axis=0, tiled=True),
        lax.all_gather(w_out, "shard", axis=0, tiled=True),
        lax.all_gather(w_small, "shard", axis=0, tiled=True),
    )
    seglens = seq_lengths[0]

    def local(resid, weight_in, weight_out, packed):
        return mixer(resid, weight_in, weight_out, packed, seglens, round_value, round_grad)

    result, pullback = jax.vjp(
        local,
        tokens.astype(jnp.float32),
        full_in.astype(jnp.float32),
        full_out.astype(jnp.float32),
        full_small.astype(jnp.float32),
    )
    places = jnp.arange(tokens.shape[0], dtype=jnp.int32)
    valid = (places < tokens.shape[0] - seglens[-1]).astype(jnp.float32)[:, None]
    grad_x, grad_in, grad_out, grad_small = pullback(cotangent.astype(jnp.float32) * valid)
    share_in, share_out, share_small = reduce_group((grad_in, grad_out, grad_small))
    new_w_in, new_m_in, new_v_in = adamw(w_in, share_in, m_in, v_in, 0.05, 0.1)
    new_w_out, new_m_out, new_v_out = adamw(w_out, share_out, m_out, v_out, 0.04, 0.1)
    new_w_small, new_m_small, new_v_small = adamw(w_small, share_small, m_small, v_small, 0.3, 0.0)
    return (
        result.astype(jnp.bfloat16),
        grad_x.astype(jnp.bfloat16),
        new_w_in,
        new_m_in,
        new_v_in,
        new_w_out,
        new_m_out,
        new_v_out,
        new_w_small,
        new_m_small,
        new_v_small,
    )


CHAN = DI + 2 * STATE
HEADS = DI // HEAD
CIN = DI + CHAN + HEADS
MAIN = DI + CHAN
PADC = MAIN + 128
T = 128
PIECES = 4
PR = 48
CH = 8
CW = 640
SROWS = 24
MESH = pl.DeviceIdType.MESH
VMEM_BYTES = 58 * 1024 * 1024
BF = jnp.bfloat16
F32 = jnp.float32


def place():
    replica, shard = lax.axis_index("replica"), lax.axis_index("shard")
    return replica // 2, replica % 2, shard // 2, shard % 2


def target(z, x, y, c):
    return (z * 2 + x, y * 2 + c)


def greet(peers):
    barrier = pltpu.get_barrier_semaphore()
    for peer in peers:
        pl.semaphore_signal(barrier, inc=1, device_id=peer, device_id_type=MESH)
    pl.semaphore_wait(barrier, len(peers))


def send(src, dst, send_sem, recv_sem, peer):
    copy = pltpu.make_async_remote_copy(
        src_ref=src, dst_ref=dst, send_sem=send_sem, recv_sem=recv_sem,
        device_id=peer, device_id_type=MESH,
    )
    copy.start()
    return copy


def gather_kernel(wi, wo, sm, fi, fo, fs, loc, s_own, r_own, s_y, r_y, s_x, r_x, s_fy, r_fy, s_fx, r_fx):
    z, x, y, c = place()
    core, other_y, other_x = target(z, x, y, 1 - c), target(z, x, 1 - y, c), target(z, 1 - x, y, c)
    greet((core, other_y, other_x))
    me, far = 2 * y + c, 2 * (1 - y) + c
    units = ((wi, fi, 96, 0, 48), (wi, fi, 96, 48, 48), (wo, fo, 192, 0, 96), (wo, fo, 192, 96, 96))
    over_y = []
    for u, (src, full, half, first, rows) in enumerate(units):
        here = pl.ds(pl.multiple_of(x * half + first, 16), rows)
        over_y.append(send(src.at[here], full.at[me, here], s_y.at[u], r_y.at[u], other_y))
    over_y.append(send(sm, fs.at[me], s_y.at[4], r_y.at[4], other_y))
    own = [
        send(src, full.at[me], s_own.at[i], r_own.at[i], core)
        for i, (src, full) in enumerate(((wi, fi), (wo, fo), (sm, fs)))
    ]
    keep = [
        pltpu.make_async_copy(src, full.at[me], loc.at[i])
        for i, (src, full) in enumerate(((wi, fi), (wo, fo), (sm, fs)))
    ]
    for copy in keep:
        copy.start()
    over_x, on_y, on_x = [], [], []
    for u, (src, full, half, first, rows) in enumerate(units):
        here = pl.ds(pl.multiple_of(x * half + first, 16), rows)
        over_y[u].wait_recv()
        part = full.at[far, here]
        over_x.append(send(part, part, s_x.at[u], r_x.at[u], other_x))
        on_y.append(send(part, part, s_fy.at[u], r_fy.at[u], core))
    over_y[4].wait_recv()
    on_y.append(send(fs.at[far], fs.at[far], s_fy.at[4], r_fy.at[4], core))
    for u, (src, full, half, first, rows) in enumerate(units):
        there = pl.ds(pl.multiple_of((1 - x) * half + first, 16), rows)
        over_x[u].wait_recv()
        part = full.at[far, there]
        on_x.append(send(part, part, s_fx.at[u], r_fx.at[u], core))
    for copy in keep:
        copy.wait()
    for copy in own + on_y + on_x:
        copy.wait_recv()
    for copy in over_y + own + over_x + on_y + on_x:
        copy.wait_send()


def gather_weights(w_in, w_out, small):
    dma = pltpu.SemaphoreType.DMA
    return pl.pallas_call(
        gather_kernel,
        out_shape=(
            jax.ShapeDtypeStruct((4, 192, CIN), BF),
            jax.ShapeDtypeStruct((4, 384, D), BF),
            jax.ShapeDtypeStruct((4, 32, 128), BF),
        ),
        in_specs=[pl.BlockSpec(memory_space=pl.ANY)] * 3,
        out_specs=[pl.BlockSpec(memory_space=pl.ANY)] * 3,
        scratch_shapes=[dma((3,)), dma((3,)), dma((3,)), dma((5,)), dma((5,)), dma((4,)), dma((4,)),
                        dma((5,)), dma((5,)), dma((4,)), dma((4,))],
        compiler_params=pltpu.CompilerParams(collective_id=0, has_side_effects=True),
        name="gather_weights",
    )(w_in, w_out, small)


def dot(a, b):
    return jnp.dot(a, b, preferred_element_type=F32)


def dot_nt(a, b):
    return lax.dot_general(a, b, (((1,), (1,)), ((), ())), preferred_element_type=F32)


def dot_tn(a, b):
    return lax.dot_general(a, b, (((0,), (0,)), ((), ())), preferred_element_type=F32)


def colsum(v):
    return jnp.sum(v, axis=0, keepdims=True)


def layer_kernel(
    x_ref, ct_ref, len_ref, wi_ref, wo_ref, taps_ref, cb_ref, head_ref, skip_ref, pg_ref, gg_ref,
    out_ref, gx_ref, g_ref, gtaps_ref, gcb_ref, ghead_ref, gskip_ref, gpg_ref, ggg_ref,
    gate, ci, conv, inner, scan, mixes, dproj, tail, nt, n2t, gated, n16, dn2_keep, dact,
):
    bounds = [len_ref[0, 0]]
    for i in range(1, 4):
        bounds.append(bounds[-1] + len_ref[0, i])
    row = lax.broadcasted_iota(jnp.int32, (T, 1), 0)
    lane = lax.broadcasted_iota(jnp.int32, (1, T), 1)

    def segment(places):
        total = jnp.zeros(places.shape, jnp.int32)
        for bound in bounds:
            total = total + (places >= bound).astype(jnp.int32)
        return total

    seg_row, seg_lane = segment(row), segment(lane)
    within = [None] + [
        ((row >= j) & (segment(row - j) == seg_row)).astype(F32) for j in range(1, KCONV)
    ]
    allowed = (seg_row == seg_lane) & (row >= lane)
    valid = (row < bounds[2]).astype(F32)

    x = x_ref[...].astype(F32)
    r1 = lax.rsqrt(jnp.mean(x * x, axis=1, keepdims=True) + epsilon)
    normed = x * r1 * pg_ref[...]
    n16[...] = normed.astype(BF)
    nt[...] = normed.T.astype(BF)
    tail[...] = jnp.zeros(tail.shape, BF)
    tail[:, :HEADS] = wi_ref[:, MAIN:]
    n = n16[...]
    step_in = dot(n, tail[...]) + head_ref[0:1, :]
    for k in range(0, DI, 512):
        gate[:, k:k + 512] = dot(n, wi_ref[:, k:k + 512])
    W = 256
    for k in range(0, CHAN, W):
        cols = slice(k, k + W)
        v = dot(n, wi_ref[:, DI + k:DI + k + W])
        ci[:, cols] = v
        total = cb_ref[:, cols] + taps_ref[KCONV - 1:KCONV, cols] * v
        for j in range(1, KCONV):
            total = total + taps_ref[KCONV - 1 - j:KCONV - j, cols] * pltpu.roll(v, j, 0) * within[j]
        conv[:, cols] = total
        inner[:, cols] = (total * jax.nn.sigmoid(total)).astype(BF)
    step = jnp.maximum(step_in, 0.0) + jnp.log1p(jnp.exp(-jnp.abs(step_in)))
    rate = -jnp.exp(head_ref[1:2, :])
    tri = (row >= lane).astype(F32)
    logs = jnp.dot(tri, step * rate, precision=lax.Precision.HIGHEST, preferred_element_type=F32)
    logs_t, step_t = logs.T, step.T
    in_state, out_state = inner[:, DI:DI + STATE], inner[:, DI + STATE:]
    inter = dot_nt(out_state, in_state)
    left = lane < HEAD
    gsq = jnp.zeros((T, 1), F32)
    for q in range(HEADS // 2):
        cols = slice(128 * q, 128 * q + 128)
        pair = inner[:, cols]
        parts = []
        for h in (2 * q, 2 * q + 1):
            spread = logs[:, h:h + 1] - logs_t[h:h + 1, :]
            decay = jnp.exp(jnp.where(allowed, spread, -1e30))
            mixes[h] = decay
            parts.append(dot((inter * decay * step_t[h:h + 1, :]).astype(BF), pair))
        value = jnp.where(left, parts[0], parts[1]) + pair.astype(F32) * skip_ref[:, cols]
        scan[:, cols] = value
        g = gate[:, cols]
        value = value * (g * jax.nn.sigmoid(g))
        gated[:, cols] = value
        gsq = gsq + jnp.sum(value * value, axis=1, keepdims=True)
    r2 = lax.rsqrt(gsq * (1.0 / DI) + epsilon)

    dy = ct_ref[...].astype(F32) * valid
    d16 = dy.astype(BF)
    out = x
    mean_ug = jnp.zeros((T, 1), F32)
    for k in range(0, DI, W):
        cols = slice(k, k + W)
        g = gated[:, cols]
        two = g * r2 * gg_ref[:, cols]
        two16 = two.astype(BF)
        n2t[cols, :] = two.T.astype(BF)
        out = out + dot(two16, wo_ref[cols, :])
        dn2 = dot_nt(d16, wo_ref[cols, :])
        ggg_ref[:, cols] = colsum(dn2 * (g * r2))
        mean_ug = mean_ug + jnp.sum(dn2 * gg_ref[:, cols] * g, axis=1, keepdims=True)
        dn2_keep[:, cols] = dn2
    out_ref[...] = out.astype(BF)
    back = mean_ug * (1.0 / DI) * r2 * r2

    dinter = jnp.zeros((T, T), F32)
    dlog = jnp.zeros((T, T), F32)
    dstep_rows, dlog_rows = [], []
    for q in range(HEADS // 2):
        cols = slice(128 * q, 128 * q + 128)
        g, value, gt = gate[:, cols], scan[:, cols], gated[:, cols]
        dgated = r2 * (dn2_keep[:, cols] * gg_ref[:, cols] - gt * back)
        sig = jax.nn.sigmoid(g)
        dscan = dgated * (g * sig)
        dproj[:, cols] = (dgated * value * (sig * (1.0 + g * (1.0 - sig)))).astype(BF)
        pair = inner[:, cols]
        pair32 = pair.astype(F32)
        gskip_ref[:, cols] = colsum(dscan * pair32)
        ds16 = dscan.astype(BF)
        parts = []
        for side, h in enumerate((2 * q, 2 * q + 1)):
            decay, srow = mixes[h], step_t[h:h + 1, :]
            mine = jnp.where(left if side == 0 else jnp.logical_not(left), pair32, 0.0).astype(BF)
            dmix = dot_nt(ds16, mine) * decay
            dinter = dinter + dmix * srow
            wide = dmix * inter
            per_source = colsum(wide)
            dstep_rows.append(per_source)
            dlog_rows.append(-per_source * srow)
            dlog = dlog + jnp.where(lane == h, jnp.sum(wide * srow, axis=1, keepdims=True), 0.0)
            parts.append(dot_tn((inter * decay * srow).astype(BF), ds16))
        dact[:, cols] = jnp.where(left, parts[0], parts[1]) + dscan * skip_ref[:, cols]
    rest = jnp.zeros((T - HEADS, T), F32)
    dstep = jnp.concatenate(dstep_rows + [rest], axis=0).T
    dlog = dlog + jnp.concatenate(dlog_rows + [rest], axis=0).T
    di16 = dinter.astype(BF)
    dact[:, DI:DI + STATE] = dot_tn(di16, out_state)
    dact[:, DI + STATE:] = dot(di16, in_state)
    upper = (row <= lane).astype(F32)
    ddecay = jnp.dot(upper, dlog, precision=lax.Precision.HIGHEST, preferred_element_type=F32)
    dstep = dstep + ddecay * rate
    draw = dstep * jax.nn.sigmoid(step_in)
    ghead_ref[0:1, :] = colsum(draw)
    ghead_ref[1:2, :] = colsum(ddecay * step * rate)
    dproj[:, MAIN:] = draw.astype(BF)
    for k in range(0, CHAN, W):
        cols = slice(k, k + W)
        v, raw = conv[:, cols], ci[:, cols]
        sig = jax.nn.sigmoid(v)
        dconv = dact[:, cols] * (sig * (1.0 + v * (1.0 - sig)))
        gcb_ref[:, cols] = colsum(dconv)
        gtaps_ref[KCONV - 1:KCONV, cols] = colsum(dconv * raw)
        dci = dconv * taps_ref[KCONV - 1:KCONV, cols]
        for j in range(1, KCONV):
            here = dconv * within[j]
            gtaps_ref[KCONV - 1 - j:KCONV - j, cols] = colsum(here * pltpu.roll(raw, j, 0))
            dci = dci + pltpu.roll(here * taps_ref[KCONV - 1 - j:KCONV - j, cols], T - j, 0)
        dproj[:, DI + k:DI + k + W] = dci.astype(BF)

    dn = dot_nt(dproj[:, MAIN:], tail[...])
    for k in range(0, MAIN, 256):
        dn = dn + dot_nt(dproj[:, k:k + 256], wi_ref[:, k:k + 256])
    xr = x * r1
    gpg_ref[...] = colsum(dn * xr)
    u = dn * pg_ref[...]
    dx = r1 * (u - xr * jnp.mean(u * xr, axis=1, keepdims=True)) + dy
    gx_ref[...] = dx.astype(BF)

    def put(shard, chunk, first, value):
        wide = value.shape[1]
        g_ref[shard, :, chunk, :, first:first + wide] = value.astype(BF).reshape(PIECES, PR, wide)

    for s in range(4):
        left_rows = nt[192 * s:192 * s + 192, :]
        for k in range(5):
            put(s, k, 0, dot(left_rows, dproj[:, CW * k:CW * k + CW]))
        put(s, 5, 0, dot(left_rows, dproj[:, 5 * CW:]))
        rows_a = n2t[384 * s:384 * s + 192, :]
        rows_b = n2t[384 * s + 192:384 * s + 384, :]
        put(s, 5, 256, dot(rows_a, d16[:, :384]))
        put(s, 6, 0, dot(rows_a, d16[:, 384:]))
        put(s, 6, 384, dot(rows_b, d16[:, :256]))
        put(s, 7, 0, dot(rows_b, d16[:, 256:]))
        put(s, 7, 512, jnp.zeros((192, 128), F32))


def layer(tokens, cotangent, lens, w_in, w_out, taps, cb, head, skip, pg, gg):
    vmem = pl.BlockSpec(memory_space=pltpu.VMEM)
    shape = jax.ShapeDtypeStruct
    return pl.pallas_call(
        layer_kernel,
        out_shape=(
            shape((T, D), BF), shape((T, D), BF), shape((4, PIECES, CH, PR, CW), BF),
            shape((KCONV, CHAN), F32), shape((1, CHAN), F32), shape((2, 128), F32),
            shape((1, DI), F32), shape((1, D), F32), shape((1, DI), F32),
        ),
        in_specs=[vmem, vmem, pl.BlockSpec(memory_space=pltpu.SMEM)] + [vmem] * 8,
        out_specs=[vmem] * 9,
        scratch_shapes=[
            pltpu.VMEM((T, DI), F32), pltpu.VMEM((T, CHAN), F32), pltpu.VMEM((T, CHAN), F32),
            pltpu.VMEM((T, CHAN), BF), pltpu.VMEM((T, DI), F32), pltpu.VMEM((HEADS, T, T), F32),
            pltpu.VMEM((T, PADC), BF), pltpu.VMEM((D, 128), BF), pltpu.VMEM((D, T), BF),
            pltpu.VMEM((DI, T), BF), pltpu.VMEM((T, DI), F32), pltpu.VMEM((T, D), BF),
            pltpu.VMEM((T, DI), F32), pltpu.VMEM((T, CHAN), F32),
        ],
        compiler_params=pltpu.CompilerParams(vmem_limit_bytes=VMEM_BYTES),
        name="layer",
    )(tokens, cotangent, lens, w_in, w_out, taps, cb, head, skip, pg, gg)


def reduce_kernel(
    g, sm, red, sm_out, own, rc, r1, r2, rz, sbuf, srecv,
    loc, s_c, r_c, s_1, r_1, s_2, r_2, s_z, r_z, s_g, r_g, s_x, r_x, s_s, r_s,
):
    z, x, y, c = place()
    core, other_y, other_x = target(z, x, y, 1 - c), target(z, x, 1 - y, c), target(z, 1 - x, y, c)
    others = [lax.rem(z + d, 4) for d in (1, 2, 3)]
    over_z = [target(o, x, y, c) for o in others]
    greet([core, other_y, other_x] + over_z)
    started = []

    def go(*args):
        copy = send(*args)
        started.append(copy)
        return copy

    mine, away = pl.ds(4 * x, 4), pl.ds(4 * (1 - x), 4)
    first = []
    small_copy = go(sm, srecv.at[0], s_s.at[0], r_s.at[0], core)
    for p in range(PIECES):
        first.append([
            go(g.at[2 * i + 1 - c, p], rc.at[i, p], s_c.at[p, i], r_c.at[p, i], core) for i in range(2)
        ])
    keep = [
        [pltpu.make_async_copy(g.at[2 * i + c, p], own.at[i, p], loc.at[p, i]) for i in range(2)]
        for p in range(PIECES)
    ]
    for pair in keep:
        for copy in pair:
            copy.start()

    def add(dst, src, chunks):
        def step(i, carry):
            a, b = dst.at[i], src.at[i]
            a[...] = (a[...].astype(F32) + b[...].astype(F32)).astype(BF)
            return carry

        lax.fori_loop(0, chunks, step, 0)

    second = []
    for p in range(PIECES):
        for i in range(2):
            keep[p][i].wait()
            first[p][i].wait_recv()
            add(own.at[i, p], rc.at[i, p], CH)
        if p % 2 == 0:
            second.append([go(own.at[1 - y, p], r1.at[p], s_1.at[p, 0], r_1.at[p, 0], other_y)])
        else:
            second.append([
                go(own.at[i, p, away], r1.at[p, pl.ds(4 * i, 4)], s_1.at[p, i], r_1.at[p, i], other_x)
                for i in range(2)
            ])
    small_copy.wait_recv()
    sbuf[0] = sm[...] + srecv[0]
    small_copy = go(sbuf.at[0], srecv.at[1], s_s.at[1], r_s.at[1], other_y)
    third = []
    for p in range(PIECES):
        for copy in second[p]:
            copy.wait_recv()
        if p % 2 == 0:
            add(own.at[y, p], r1.at[p], CH)
            third.append(go(own.at[y, p, away], r2.at[p], s_2.at[p], r_2.at[p], other_x))
        else:
            for i in range(2):
                add(own.at[i, p, mine], r1.at[p, pl.ds(4 * i, 4)], 4)
            third.append(go(own.at[1 - y, p, mine], r2.at[p], s_2.at[p], r_2.at[p], other_y))
    small_copy.wait_recv()
    sbuf[1] = sbuf[0] + srecv[1]
    small_copy = go(sbuf.at[1], srecv.at[2], s_s.at[2], r_s.at[2], other_x)
    spread = []
    for p in range(PIECES):
        third[p].wait_recv()
        add(own.at[y, p, mine], r2.at[p], 4)
        spread.append([
            go(own.at[y, p, 4 * x + others[d]], rz.at[p, d], s_z.at[p, d], r_z.at[p, d], over_z[d])
            for d in range(3)
        ])
    small_copy.wait_recv()
    sbuf[2] = sbuf[1] + srecv[2]
    small = [go(sbuf.at[2], srecv.at[3 + d], s_s.at[3 + d], r_s.at[3 + d], over_z[d]) for d in range(3)]
    back = []
    for p in range(PIECES):
        for copy in spread[p]:
            copy.wait_recv()
        total = own[y, p, 4 * x + z].astype(F32)
        for d in range(3):
            total = total + rz[p, d].astype(F32)
        at = red.at[p, 4 * x + z]
        at[...] = total.astype(BF)
        back.append([go(at, at, s_g.at[p, d], r_g.at[p, d], over_z[d]) for d in range(3)])
    last = []
    for p in range(PIECES):
        for copy in back[p]:
            copy.wait_recv()
        at = red.at[p, mine]
        last.append(go(at, at, s_x.at[p], r_x.at[p], other_x))
    for copy in small:
        copy.wait_recv()
    pieces = [sbuf[2], srecv[3], srecv[4], srecv[5]]
    here = jnp.zeros(here_shape, F32)
    for zi in range(4):
        back_by = lax.rem(z - zi + 4, 4)
        pick = pieces[0]
        for d in (1, 2, 3):
            pick = jnp.where(back_by == d, pieces[d], pick)
        here = here + pick
    mine_rows = jnp.where(y == 0, jnp.where(c == 0, here[0], here[1]), jnp.where(c == 0, here[2], here[3]))
    sm_out[...] = mine_rows
    for copy in last:
        copy.wait_recv()
    for copy in started:
        copy.wait_send()


here_shape = (4, SROWS, 128)


def reduce_grads(g, small):
    dma = pltpu.SemaphoreType.DMA
    vmem = pl.BlockSpec(memory_space=pltpu.VMEM)
    return pl.pallas_call(
        reduce_kernel,
        out_shape=(
            jax.ShapeDtypeStruct((PIECES, CH, PR, CW), BF),
            jax.ShapeDtypeStruct((SROWS, 128), F32),
        ),
        in_specs=[pl.BlockSpec(memory_space=pl.ANY), vmem],
        out_specs=[vmem, vmem],
        scratch_shapes=[
            pltpu.VMEM((2, PIECES, CH, PR, CW), BF), pltpu.VMEM((2, PIECES, CH, PR, CW), BF),
            pltpu.VMEM((PIECES, CH, PR, CW), BF), pltpu.VMEM((PIECES, 4, PR, CW), BF),
            pltpu.VMEM((PIECES, 3, PR, CW), BF),
            pltpu.VMEM((3, 4, SROWS, 128), F32), pltpu.VMEM((6, 4, SROWS, 128), F32),
            dma((PIECES, 2)), dma((PIECES, 2)), dma((PIECES, 2)), dma((PIECES, 2)), dma((PIECES, 2)),
            dma((PIECES,)), dma((PIECES,)), dma((PIECES, 3)), dma((PIECES, 3)), dma((PIECES, 3)),
            dma((PIECES, 3)), dma((PIECES,)), dma((PIECES,)), dma((6,)), dma((6,)),
        ],
        compiler_params=pltpu.CompilerParams(
            collective_id=1, has_side_effects=True, vmem_limit_bytes=VMEM_BYTES
        ),
        name="reduce_grads",
    )(g, small)


def adamw_kernel(red, wi, mi, vi, wo, mo, vo, nwi, nmi, nvi, nwo, nmo, nvo):
    def update(cols, grad, refs, rate, part=None):
        at = (slice(None), cols) if part is None else (part, slice(None), cols)
        new = adamw(refs[0][at], grad.astype(F32), refs[1][at], refs[2][at], rate, 0.1)
        for ref, value in zip(refs[3:], new):
            ref[at] = value

    refs_in = (wi, mi, vi, nwi, nmi, nvi)
    refs_out = (wo, mo, vo, nwo, nmo, nvo)
    for k in range(5):
        update(slice(CW * k, CW * k + CW), red[0, k], refs_in, 0.05)
    update(slice(5 * CW, CIN), red[0, 5, :, :CIN - 5 * CW], refs_in, 0.05)
    update(slice(0, 384), red[0, 5, :, 256:], refs_out, 0.04, 0)
    update(slice(384, 768), red[0, 6, :, :384], refs_out, 0.04, 0)
    update(slice(0, 256), red[0, 6, :, 384:], refs_out, 0.04, 1)
    update(slice(256, 768), red[0, 7, :, :512], refs_out, 0.04, 1)


def adamw_all(red, w_in, m_in, v_in, w_out, m_out, v_out):
    rows = 16
    halves = [v.reshape(2, 192, D) for v in (w_out, m_out, v_out)]
    spec_in = pl.BlockSpec((rows, CIN), lambda i: (i, 0))
    spec_out = pl.BlockSpec((2, rows, D), lambda i: (0, i, 0))
    new = pl.pallas_call(
        adamw_kernel,
        grid=(192 // rows,),
        out_shape=[jax.ShapeDtypeStruct((192, CIN), F32)] * 3 + [jax.ShapeDtypeStruct((2, 192, D), F32)] * 3,
        in_specs=[pl.BlockSpec((1, CH, rows, CW), lambda i: (i // 3, 0, i % 3, 0))]
        + [spec_in] * 3 + [spec_out] * 3,
        out_specs=[spec_in] * 3 + [spec_out] * 3,
        compiler_params=pltpu.CompilerParams(vmem_limit_bytes=VMEM_BYTES),
        name="adamw",
    )(red, w_in, m_in, v_in, *halves)
    return list(new[:3]) + [v.reshape(384, D) for v in new[3:]]


def on_device_fast(
    tokens, cotangent, seq_lengths, w_in, w_out, w_small, m_in, v_in, m_out, v_out, m_small, v_small
):
    share = w_small.shape[0]
    small = jnp.pad(w_small, (0, 32 * 128 - share)).reshape(32, 128)
    full_in, full_out, full_small = gather_weights(w_in, w_out, small)
    packed = full_small.reshape(4, 32 * 128)[:, :share].reshape(4 * share).astype(F32)
    start = (KCONV + 1) * CHAN
    taps = packed[: KCONV * CHAN].reshape(KCONV, CHAN)
    cb = packed[KCONV * CHAN : start].reshape(1, CHAN)
    head = jnp.pad(packed[start : start + 2 * HEADS].reshape(2, HEADS), ((0, 0), (0, 128 - HEADS)))
    skip = jnp.repeat(packed[start + 2 * HEADS : start + 3 * HEADS], HEAD).reshape(1, DI)
    gains = start + 3 * HEADS
    pg = packed[gains : gains + D].reshape(1, D)
    gg = packed[gains + D :].reshape(1, DI)
    out, gx, g, gtaps, gcb, ghead, gskip, gpg, ggg = layer(
        tokens, cotangent, seq_lengths, full_in.reshape(D, CIN), full_out.reshape(DI, D),
        taps, cb, head, skip, pg, gg,
    )
    flat = jnp.concatenate([
        gtaps.reshape(-1), gcb.reshape(-1), ghead[:, :HEADS].reshape(-1),
        gskip.reshape(HEADS, HEAD).sum(axis=1), gpg.reshape(-1), ggg.reshape(-1),
    ])
    flat = jnp.pad(flat.reshape(4, share), ((0, 0), (0, SROWS * 128 - share))).reshape(4, SROWS, 128)
    red, small_sum = reduce_grads(g, flat)
    new = adamw_all(red, w_in, m_in, v_in, w_out, m_out, v_out)
    share_small = small_sum.reshape(-1)[:share]
    new_small = adamw(w_small, share_small, m_small, v_small, 0.3, 0.0)
    return (out, gx, *new, *new_small)


def solution(mesh):
    in_specs = (
        P(("replica", "shard"), None),
        P(("replica", "shard"), None),
        P(("replica", "shard"), None),
        P("shard", None),
        P("shard", None),
        P("shard"),
        P("shard", None),
        P("shard", None),
        P("shard", None),
        P("shard", None),
        P("shard"),
        P("shard"),
    )
    out_specs = (
        P(("replica", "shard"), None),
        P(("replica", "shard"), None),
        P("shard", None),
        P("shard", None),
        P("shard", None),
        P("shard", None),
        P("shard", None),
        P("shard", None),
        P("shard"),
        P("shard"),
        P("shard"),
    )
    fast = dict(mesh.shape) == {"replica": 8, "shard": 4}
    return jax.shard_map(
        on_device_fast if fast else on_device, mesh=mesh, in_specs=in_specs, out_specs=out_specs, check_vma=False
    )
```

```python
import jax
import jax.numpy as jnp
from jax import lax
from jax.experimental import pallas as pl
from jax.experimental.pallas import tpu as pltpu
from jax.sharding import PartitionSpec as P

D = 768
STATE = 128
HEAD = 64
KCONV = 4
STEP = 10
DI = 1536


epsilon = 1e-05
beta_one = 0.9
beta_two = 0.95
adam_eps = 1e-08


def make_rounders():

    def round_plain(value):
        return lax.optimization_barrier(value.astype(jnp.bfloat16)).astype(jnp.float32)

    def unchanged(value):
        return value

    round_value = jax.custom_vjp(round_plain)
    round_grad = jax.custom_vjp(unchanged)

    def value_keep(value):
        return (round_plain(value), None)

    def value_pass(kept, gradient):
        return (gradient,)

    def grad_keep(value):
        return (value, None)

    def grad_round(kept, gradient):
        return (round_plain(gradient),)

    round_value.defvjp(value_keep, value_pass)
    round_grad.defvjp(grad_keep, grad_round)
    return (round_value, round_grad)


def mixer(resid, weight_in, weight_out, packed, seglens, round_value, round_grad):
    rows_count = resid.shape[0]
    channels = DI + 2 * STATE
    heads = DI // HEAD
    kernel = packed[: KCONV * channels].reshape(KCONV, channels)
    conv_bias = packed[KCONV * channels : (KCONV + 1) * channels]
    start = (KCONV + 1) * channels
    step_bias = packed[start : start + heads]
    decay_log = packed[start + heads : start + 2 * heads]
    skip_gain = packed[start + 2 * heads : start + 3 * heads]
    pre_gain = packed[start + 3 * heads : start + 3 * heads + D]
    gate_gain = packed[start + 3 * heads + D :]
    places = jnp.arange(rows_count, dtype=jnp.int32)
    bounds = jnp.cumsum(seglens)
    segment = jnp.sum((places[:, None] >= bounds[None, :]).astype(jnp.int32), axis=1)
    meansq = jnp.mean(resid * resid, axis=1, keepdims=True)
    normed = resid * lax.rsqrt(meansq + epsilon) * pre_gain
    project = round_grad(
        jnp.dot(round_value(normed), weight_in, preferred_element_type=jnp.float32)
    )
    gate_raw = project[:, :DI]
    conv_in = project[:, DI : DI + channels]
    step_raw = project[:, DI + channels :]
    convolved = conv_bias + kernel[KCONV - 1] * conv_in
    for offset in range(1, KCONV):
        shifted = jnp.concatenate(
            [jnp.zeros((offset, channels), jnp.float32), conv_in[:-offset]], axis=0
        )
        earlier = jnp.concatenate([jnp.full((offset,), -1, jnp.int32), segment[:-offset]])
        within = (earlier == segment).astype(jnp.float32)[:, None]
        convolved = convolved + kernel[KCONV - 1 - offset] * shifted * within
    activated = jax.nn.silu(convolved)
    inner = round_value(activated[:, :DI])
    in_state = round_value(activated[:, DI : DI + STATE])
    out_state = round_value(activated[:, DI + STATE :])
    step_size = jax.nn.softplus(step_raw + step_bias)
    logrates = jnp.cumsum(step_size * -jnp.exp(decay_log), axis=0)
    intersection = round_grad(jnp.dot(out_state, in_state.T, preferred_element_type=jnp.float32))
    allowed = (segment[:, None] == segment[None, :]) & (places[:, None] >= places[None, :])
    group_count = heads // 8
    rates_grouped = logrates.reshape(rows_count, group_count, 8).transpose(1, 0, 2)
    steps_grouped = step_size.reshape(rows_count, group_count, 8).transpose(1, 0, 2)
    inner_grouped = inner.reshape(rows_count, group_count, 8, HEAD).transpose(1, 0, 2, 3)

    def mix_group(entry):
        rate_part, step_part, inner_part = entry
        spread = rate_part.T[:, :, None] - rate_part.T[:, None, :]
        weights = round_value(
            intersection[None]
            * jnp.exp(jnp.where(allowed[None], spread, -1e30))
            * step_part.T[:, None, :]
        )
        return jnp.einsum("hts,shp->thp", weights, inner_part, preferred_element_type=jnp.float32)

    mixed = lax.map(jax.checkpoint(mix_group), (rates_grouped, steps_grouped, inner_grouped))
    scanned = round_grad(mixed.transpose(1, 0, 2, 3).reshape(rows_count, DI)) + inner * jnp.repeat(
        skip_gain, HEAD
    )
    gated = scanned * jax.nn.silu(gate_raw)
    gatesq = jnp.mean(gated * gated, axis=1, keepdims=True)
    normed_two = gated * lax.rsqrt(gatesq + epsilon) * gate_gain
    output = round_grad(
        jnp.dot(round_value(normed_two), weight_out, preferred_element_type=jnp.float32)
    )
    return resid + output


def adamw(weight, gradient, first, second, rate, decay):
    first_new = beta_one * first + (1.0 - beta_one) * gradient
    second_new = beta_two * second + (1.0 - beta_two) * gradient * gradient
    corrected = (
        first_new
        / (1.0 - beta_one**STEP)
        / (jnp.sqrt(second_new / (1.0 - beta_two**STEP)) + adam_eps)
    )
    master = weight.astype(jnp.float32)
    return (master - rate * (corrected + decay * master), first_new, second_new)


def reduce_group(grads):
    shares = (
        lax.psum_scatter(grads[0], "shard", scatter_dimension=0, tiled=True),
        lax.psum_scatter(grads[1], "shard", scatter_dimension=0, tiled=True),
        lax.psum_scatter(grads[2], "shard", scatter_dimension=0, tiled=True),
    )
    return lax.psum((shares[0], shares[1], shares[2]), "replica")


def on_device(
    tokens, cotangent, seq_lengths, w_in, w_out, w_small, m_in, v_in, m_out, v_out, m_small, v_small
):
    round_value, round_grad = make_rounders()
    full_in, full_out, full_small = (
        lax.all_gather(w_in, "shard", axis=0, tiled=True),
        lax.all_gather(w_out, "shard", axis=0, tiled=True),
        lax.all_gather(w_small, "shard", axis=0, tiled=True),
    )
    seglens = seq_lengths[0]

    def local(resid, weight_in, weight_out, packed):
        return mixer(resid, weight_in, weight_out, packed, seglens, round_value, round_grad)

    result, pullback = jax.vjp(
        local,
        tokens.astype(jnp.float32),
        full_in.astype(jnp.float32),
        full_out.astype(jnp.float32),
        full_small.astype(jnp.float32),
    )
    places = jnp.arange(tokens.shape[0], dtype=jnp.int32)
    valid = (places < tokens.shape[0] - seglens[-1]).astype(jnp.float32)[:, None]
    grad_x, grad_in, grad_out, grad_small = pullback(cotangent.astype(jnp.float32) * valid)
    share_in, share_out, share_small = reduce_group((grad_in, grad_out, grad_small))
    new_w_in, new_m_in, new_v_in = adamw(w_in, share_in, m_in, v_in, 0.05, 0.1)
    new_w_out, new_m_out, new_v_out = adamw(w_out, share_out, m_out, v_out, 0.04, 0.1)
    new_w_small, new_m_small, new_v_small = adamw(w_small, share_small, m_small, v_small, 0.3, 0.0)
    return (
        result.astype(jnp.bfloat16),
        grad_x.astype(jnp.bfloat16),
        new_w_in,
        new_m_in,
        new_v_in,
        new_w_out,
        new_m_out,
        new_v_out,
        new_w_small,
        new_m_small,
        new_v_small,
    )


CHAN = DI + 2 * STATE
HEADS = DI // HEAD
CIN = DI + CHAN + HEADS
MAIN = DI + CHAN
PADC = MAIN + 128
T = 128
PIECES = 4
PR = 48
CH = 8
CW = 640
SROWS = 24
MESH = pl.DeviceIdType.MESH
VMEM_BYTES = 58 * 1024 * 1024
BF = jnp.bfloat16
F32 = jnp.float32


def place():
    replica, shard = lax.axis_index("replica"), lax.axis_index("shard")
    return replica // 2, replica % 2, shard // 2, shard % 2


def target(z, x, y, c):
    return (z * 2 + x, y * 2 + c)


def greet(peers):
    barrier = pltpu.get_barrier_semaphore()
    for peer in peers:
        pl.semaphore_signal(barrier, inc=1, device_id=peer, device_id_type=MESH)
    pl.semaphore_wait(barrier, len(peers))


def send(src, dst, send_sem, recv_sem, peer):
    copy = pltpu.make_async_remote_copy(
        src_ref=src, dst_ref=dst, send_sem=send_sem, recv_sem=recv_sem,
        device_id=peer, device_id_type=MESH,
    )
    copy.start()
    return copy


def gather_kernel(wi, sm, fi, fs, loc, s_own, r_own, s_y, r_y, s_x, r_x, s_fy, r_fy, s_fx, r_fx):
    z, x, y, c = place()
    core, other_y, other_x = target(z, x, y, 1 - c), target(z, x, 1 - y, c), target(z, 1 - x, y, c)
    greet((core, other_y, other_x))
    me, far = 2 * y + c, 2 * (1 - y) + c
    over_y = [send(sm, fs.at[me], s_y.at[3], r_y.at[3], other_y)]
    own = [send(sm, fs.at[me], s_own.at[1], r_own.at[1], core)]
    for u in range(3):
        here = pl.ds(pl.multiple_of(x * 96 + 32 * u, 16), 32)
        over_y.append(send(wi.at[here], fi.at[me, here], s_y.at[u], r_y.at[u], other_y))
    own.append(send(wi, fi.at[me], s_own.at[0], r_own.at[0], core))
    keep = [
        pltpu.make_async_copy(src, full.at[me], loc.at[i])
        for i, (src, full) in enumerate(((wi, fi), (sm, fs)))
    ]
    for copy in keep:
        copy.start()
    over_x, on_y, on_x = [], [], []
    over_y[0].wait_recv()
    on_y.append(send(fs.at[far], fs.at[far], s_fy.at[3], r_fy.at[3], core))
    for u in range(3):
        here = pl.ds(pl.multiple_of(x * 96 + 32 * u, 16), 32)
        over_y[u + 1].wait_recv()
        part = fi.at[far, here]
        over_x.append(send(part, part, s_x.at[u], r_x.at[u], other_x))
        on_y.append(send(part, part, s_fy.at[u], r_fy.at[u], core))
    for u in range(3):
        there = pl.ds(pl.multiple_of((1 - x) * 96 + 32 * u, 16), 32)
        over_x[u].wait_recv()
        part = fi.at[far, there]
        on_x.append(send(part, part, s_fx.at[u], r_fx.at[u], core))
    for copy in keep:
        copy.wait()
    for copy in own + on_y + on_x:
        copy.wait_recv()
    for copy in over_y + own + over_x + on_y + on_x:
        copy.wait_send()


def gather_weights(w_in, small):
    dma = pltpu.SemaphoreType.DMA
    return pl.pallas_call(
        gather_kernel,
        out_shape=(
            jax.ShapeDtypeStruct((4, 192, CIN), BF),
            jax.ShapeDtypeStruct((4, 32, 128), BF),
        ),
        in_specs=[pl.BlockSpec(memory_space=pl.ANY)] * 2,
        out_specs=[pl.BlockSpec(memory_space=pl.ANY)] * 2,
        scratch_shapes=[dma((2,)), dma((2,)), dma((2,)), dma((4,)), dma((4,)), dma((3,)), dma((3,)),
                        dma((4,)), dma((4,)), dma((3,)), dma((3,))],
        compiler_params=pltpu.CompilerParams(collective_id=0, has_side_effects=True),
        name="gather_weights",
    )(w_in, small)


def dot(a, b):
    return jnp.dot(a, b, preferred_element_type=F32)


def dot_nt(a, b):
    return lax.dot_general(a, b, (((1,), (1,)), ((), ())), preferred_element_type=F32)


def dot_tn(a, b):
    return lax.dot_general(a, b, (((0,), (0,)), ((), ())), preferred_element_type=F32)


def colsum(v):
    return jnp.sum(v, axis=0, keepdims=True)


def layer_kernel(
    x_ref, ct_ref, len_ref, wi_ref, wo_own, par_ref,
    out_ref, gx_ref, red, sm_out,
    gate, ci, conv, inner, scan, mixes, dproj, tail, nt, n2t, gated, n16, dn2_keep, dact,
    wo_full, d_own, d_in, n_in, n2_in, dp_in, own, half_in, rz, gs, sbuf, srecv,
    s_w, r_w, s_d, r_d, s_n, r_n, s_2, r_2, s_p, r_p, s_h, r_h, s_z, r_z, s_g, r_g, s_x, r_x, s_s, r_s,
):
    z, x_at, y, c = place()
    core, other_y = target(z, x_at, y, 1 - c), target(z, x_at, 1 - y, c)
    diag, other_x = target(z, x_at, 1 - y, 1 - c), target(z, 1 - x_at, y, c)
    others = [lax.rem(z + d, 4) for d in (1, 2, 3)]
    over_z = [target(o, x_at, y, c) for o in others]
    greet([core, other_y, diag, other_x] + over_z)
    started = []

    def go(*args):
        copy = send(*args)
        started.append(copy)
        return copy

    me, far = 2 * y + c, 2 * (1 - y) + c
    group = [(core, 2 * y + 1 - c), (other_y, far), (diag, 2 * (1 - y) + 1 - c)]
    here = pl.ds(pl.multiple_of(x_at * 192, 16), 192)
    there = pl.ds(pl.multiple_of((1 - x_at) * 192, 16), 192)
    w_over_y = go(wo_own.at[here], wo_full.at[me, here], s_w.at[0], r_w.at[0], other_y)
    w_own = go(wo_own, wo_full.at[me], s_w.at[1], r_w.at[1], core)
    wo_full[me] = wo_own[...]
    taps_ref, cb_ref = par_ref.at[0:4], par_ref.at[4:5]
    pg_ref, gg_ref = par_ref.at[5:6, 0:D], par_ref.at[6:7, 0:DI]
    step_bias, decay_log, skips = (par_ref[5:6, 768 + 128 * i:896 + 128 * i] for i in range(3))
    gs[...] = jnp.zeros(gs.shape, F32)
    bounds = [len_ref[0, 0]]
    for i in range(1, 4):
        bounds.append(bounds[-1] + len_ref[0, i])
    row = lax.broadcasted_iota(jnp.int32, (T, 1), 0)
    lane = lax.broadcasted_iota(jnp.int32, (1, T), 1)

    def segment(places):
        total = jnp.zeros(places.shape, jnp.int32)
        for bound in bounds:
            total = total + (places >= bound).astype(jnp.int32)
        return total

    seg_row, seg_lane = segment(row), segment(lane)
    within = [None] + [
        ((row >= j) & (segment(row - j) == seg_row)).astype(F32) for j in range(1, KCONV)
    ]
    allowed = (seg_row == seg_lane) & (row >= lane)
    valid = (row < bounds[2]).astype(F32)

    x = x_ref[...].astype(F32)
    r1 = lax.rsqrt(jnp.mean(x * x, axis=1, keepdims=True) + epsilon)
    normed = x * r1 * pg_ref[...]
    n16[...] = normed.astype(BF)
    nt[...] = normed.T.astype(BF).reshape(4, 192, T)
    dy = ct_ref[...].astype(F32) * valid
    d16 = dy.astype(BF)
    d_own[...] = d16
    d_got, n_got, n2_got = [], [], []
    for i, (peer, shard) in enumerate(group):
        n_got.append(go(nt.at[shard], n_in.at[i], s_n.at[i], r_n.at[i], peer))
        d_got.append(go(d_own, d_in.at[i], s_d.at[i], r_d.at[i], peer))
    tail[...] = jnp.zeros(tail.shape, BF)
    tail[:, :HEADS] = wi_ref[:, MAIN:]
    n = n16[...]
    step_in = dot(n, tail[...]) + step_bias
    for k in range(0, DI, 512):
        gate[:, k:k + 512] = dot(n, wi_ref[:, k:k + 512])
    W = 256
    for k in range(0, CHAN, W):
        cols = slice(k, k + W)
        v = dot(n, wi_ref[:, DI + k:DI + k + W])
        ci[:, cols] = v
        total = cb_ref[:, cols] + taps_ref[KCONV - 1:KCONV, cols] * v
        for j in range(1, KCONV):
            total = total + taps_ref[KCONV - 1 - j:KCONV - j, cols] * pltpu.roll(v, j, 0) * within[j]
        conv[:, cols] = total
        inner[:, cols] = (total * jax.nn.sigmoid(total)).astype(BF)
    w_over_y.wait_recv()
    part = wo_full.at[far, here]
    w_over_x = go(part, part, s_w.at[2], r_w.at[2], other_x)
    w_fwd = go(part, part, s_w.at[3], r_w.at[3], core)
    step = jnp.maximum(step_in, 0.0) + jnp.log1p(jnp.exp(-jnp.abs(step_in)))
    rate = -jnp.exp(decay_log)
    tri = (row >= lane).astype(F32)
    logs = jnp.dot(tri, step * rate, precision=lax.Precision.HIGHEST, preferred_element_type=F32)
    logs_t, step_t = logs.T, step.T
    in_state, out_state = inner[:, DI:DI + STATE], inner[:, DI + STATE:]
    inter = dot_nt(out_state, in_state)
    left = lane < HEAD

    def skip_of(q):
        return jnp.where(left, skips[:, 2 * q:2 * q + 1], skips[:, 2 * q + 1:2 * q + 2])

    gsq = jnp.zeros((T, 1), F32)
    for q in range(HEADS // 2):
        cols = slice(128 * q, 128 * q + 128)
        pair = inner[:, cols]
        parts = []
        for h in (2 * q, 2 * q + 1):
            spread = logs[:, h:h + 1] - logs_t[h:h + 1, :]
            decay = jnp.exp(jnp.where(allowed, spread, -1e30))
            mixes[h] = decay
            parts.append(dot((inter * decay * step_t[h:h + 1, :]).astype(BF), pair))
        value = jnp.where(left, parts[0], parts[1]) + pair.astype(F32) * skip_of(q)
        scan[:, cols] = value
        g = gate[:, cols]
        value = value * (g * jax.nn.sigmoid(g))
        gated[:, cols] = value
        gsq = gsq + jnp.sum(value * value, axis=1, keepdims=True)
    r2 = lax.rsqrt(gsq * (1.0 / DI) + epsilon)

    w_over_x.wait_recv()
    part = wo_full.at[far, there]
    w_last = go(part, part, s_w.at[4], r_w.at[4], core)
    for copy in (w_own, w_fwd, w_last):
        copy.wait_recv()
    out = x
    mean_ug = jnp.zeros((T, 1), F32)
    W = 128
    for k in range(0, DI, W):
        cols = slice(k, k + W)
        g = gated[:, cols]
        two = g * r2 * gg_ref[:, cols]
        two16 = two.astype(BF)
        w_part = wo_full[k // 384, k % 384:k % 384 + W, :]
        n2t[k // 384, k % 384:k % 384 + W, :] = two.T.astype(BF)
        out = out + dot(two16, w_part)
        dn2 = dot_nt(d16, w_part)
        gs[6:7, cols] = colsum(dn2 * (g * r2))
        mean_ug = mean_ug + jnp.sum(dn2 * gg_ref[:, cols] * g, axis=1, keepdims=True)
        dn2_keep[:, cols] = dn2
    out_ref[...] = out.astype(BF)
    for i, (peer, shard) in enumerate(group):
        n2_got.append(go(n2t.at[shard], n2_in.at[i], s_2.at[i], r_2.at[i], peer))
    back = mean_ug * (1.0 / DI) * r2 * r2

    dinter = jnp.zeros((T, T), F32)
    dlog = jnp.zeros((T, T), F32)
    dskip = jnp.zeros((1, T), F32)
    dstep_rows, dlog_rows = [], []
    for q in range(HEADS // 2):
        cols = slice(128 * q, 128 * q + 128)
        g, value, gt = gate[:, cols], scan[:, cols], gated[:, cols]
        dgated = r2 * (dn2_keep[:, cols] * gg_ref[:, cols] - gt * back)
        sig = jax.nn.sigmoid(g)
        dscan = dgated * (g * sig)
        dproj[:, cols] = (dgated * value * (sig * (1.0 + g * (1.0 - sig)))).astype(BF)
        pair = inner[:, cols]
        pair32 = pair.astype(F32)
        by_lane = colsum(dscan * pair32)
        ds16 = dscan.astype(BF)
        parts = []
        for side, h in enumerate((2 * q, 2 * q + 1)):
            decay, srow = mixes[h], step_t[h:h + 1, :]
            mine = jnp.where(left if side == 0 else jnp.logical_not(left), pair32, 0.0).astype(BF)
            dmix = dot_nt(ds16, mine) * decay
            half = jnp.where(left if side == 0 else jnp.logical_not(left), by_lane, 0.0)
            dskip = dskip + jnp.where(lane == h, jnp.sum(half, axis=1, keepdims=True), 0.0)
            dinter = dinter + dmix * srow
            wide = dmix * inter
            per_source = colsum(wide)
            dstep_rows.append(per_source)
            dlog_rows.append(-per_source * srow)
            dlog = dlog + jnp.where(lane == h, jnp.sum(wide * srow, axis=1, keepdims=True), 0.0)
            parts.append(dot_tn((inter * decay * srow).astype(BF), ds16))
        dact[:, cols] = jnp.where(left, parts[0], parts[1]) + dscan * skip_of(q)
    def spread_dproj(part, cols):
        return [
            go(dproj.at[:, cols], dp_in.at[i, :, cols], s_p.at[part, i], r_p.at[part, i], group[i][0])
            for i in range(2)
        ]

    dp_got = [spread_dproj(0, pl.ds(0, DI))]
    rest = jnp.zeros((T - HEADS, T), F32)
    dstep = jnp.concatenate(dstep_rows + [rest], axis=0).T
    dlog = dlog + jnp.concatenate(dlog_rows + [rest], axis=0).T
    di16 = dinter.astype(BF)
    dact[:, DI:DI + STATE] = dot_tn(di16, out_state)
    dact[:, DI + STATE:] = dot(di16, in_state)
    upper = (row <= lane).astype(F32)
    ddecay = jnp.dot(upper, dlog, precision=lax.Precision.HIGHEST, preferred_element_type=F32)
    dstep = dstep + ddecay * rate
    draw = dstep * jax.nn.sigmoid(step_in)
    gs[5:6, 768:896] = colsum(draw)
    gs[5:6, 896:1024] = colsum(ddecay * step * rate)
    gs[5:6, 1024:1152] = dskip
    dproj[:, MAIN:] = draw.astype(BF)
    W = 256
    for k in range(0, CHAN, W):
        cols = slice(k, k + W)
        v, raw = conv[:, cols], ci[:, cols]
        sig = jax.nn.sigmoid(v)
        dconv = dact[:, cols] * (sig * (1.0 + v * (1.0 - sig)))
        gs[4:5, cols] = colsum(dconv)
        gs[KCONV - 1:KCONV, cols] = colsum(dconv * raw)
        dci = dconv * taps_ref[KCONV - 1:KCONV, cols]
        for j in range(1, KCONV):
            here = dconv * within[j]
            gs[KCONV - 1 - j:KCONV - j, cols] = colsum(here * pltpu.roll(raw, j, 0))
            dci = dci + pltpu.roll(here * taps_ref[KCONV - 1 - j:KCONV - j, cols], T - j, 0)
        dproj[:, DI + k:DI + k + W] = dci.astype(BF)

    dp_got.append(spread_dproj(1, pl.ds(DI, PADC - DI)))
    dn = dot_nt(dproj[:, MAIN:], tail[...])
    for k in range(0, MAIN, 256):
        dn = dn + dot_nt(dproj[:, k:k + 256], wi_ref[:, k:k + 256])
    xr = x * r1
    gs[5:6, 0:D] = colsum(dn * xr)
    u = dn * pg_ref[...]
    dx = r1 * (u - xr * jnp.mean(u * xr, axis=1, keepdims=True)) + dy
    gx_ref[...] = dx.astype(BF)

    small_copy = go(gs, srecv.at[0], s_s.at[0], r_s.at[0], core)
    forwarded = []
    for part, cols in enumerate((pl.ds(0, DI), pl.ds(DI, PADC - DI))):
        dp_got[part][1].wait_recv()
        forwarded.append(go(
            dp_in.at[1, :, cols], dp_in.at[2, :, cols], s_p.at[part, 2], r_p.at[part, 2], core
        ))
        dp_got[part][0].wait_recv()
    for copy in n_got + d_got + n2_got:
        copy.wait_recv()
    n_all = [nt[me]] + [n_in[i] for i in range(3)]
    n2_all = [n2t[me]] + [n2_in[i] for i in range(3)]
    d_all = [d_own] + [d_in.at[i] for i in range(3)]
    dp_all = [dproj] + [dp_in.at[i] for i in range(3)]

    def put(chunk, first, value):
        wide = value.shape[1]
        own[:, chunk, :, first:first + wide] = value.astype(BF).reshape(PIECES, PR, wide)

    def total(lefts, rights, cols):
        value = dot(lefts[0], rights[0][:, cols])
        for a, b in zip(lefts[1:], rights[1:]):
            value = value + dot(a, b[:, cols])
        return value

    rows_a, rows_b = [v[:192] for v in n2_all], [v[192:] for v in n2_all]
    put(5, 256, total(rows_a, d_all, slice(0, 384)))
    put(6, 0, total(rows_a, d_all, slice(384, 768)))
    put(6, 384, total(rows_b, d_all, slice(0, 256)))
    put(7, 0, total(rows_b, d_all, slice(256, 768)))
    put(7, 512, jnp.zeros((192, 128), F32))
    small_copy.wait_recv()
    sbuf[0] = gs[...] + srecv[0]
    small_copy = go(sbuf.at[0], srecv.at[1], s_s.at[1], r_s.at[1], other_y)
    forwarded[0].wait_recv()
    for k in range(2):
        put(k, 0, total(n_all, dp_all, slice(CW * k, CW * k + CW)))
    forwarded[1].wait_recv()
    for k in range(2, 5):
        put(k, 0, total(n_all, dp_all, slice(CW * k, CW * k + CW)))
    put(5, 0, total(n_all, dp_all, slice(5 * CW, PADC)))

    mine, away = pl.ds(4 * x_at, 4), pl.ds(4 * (1 - x_at), 4)
    halves = [go(own.at[p, away], half_in.at[p], s_h.at[p], r_h.at[p], other_x) for p in range(PIECES)]
    small_copy.wait_recv()
    sbuf[1] = sbuf[0] + srecv[1]
    small_copy = go(sbuf.at[1], srecv.at[2], s_s.at[2], r_s.at[2], other_x)
    spread = []
    for p in range(PIECES):
        halves[p].wait_recv()
        for i in range(4):
            at = own.at[p, 4 * x_at + i]
            at[...] = (at[...].astype(F32) + half_in[p, i].astype(F32)).astype(BF)
        spread.append([
            go(own.at[p, 4 * x_at + others[d]], rz.at[p, d], s_z.at[p, d], r_z.at[p, d], over_z[d])
            for d in range(3)
        ])
    small_copy.wait_recv()
    sbuf[2] = sbuf[1] + srecv[2]
    small = [go(sbuf.at[2], srecv.at[3 + d], s_s.at[3 + d], r_s.at[3 + d], over_z[d]) for d in range(3)]
    back = []
    for p in range(PIECES):
        for copy in spread[p]:
            copy.wait_recv()
        value = own[p, 4 * x_at + z].astype(F32)
        for d in range(3):
            value = value + rz[p, d].astype(F32)
        at = red.at[p, 4 * x_at + z]
        at[...] = value.astype(BF)
        back.append([go(at, at, s_g.at[p, d], r_g.at[p, d], over_z[d]) for d in range(3)])
    last = []
    for p in range(PIECES):
        for copy in back[p]:
            copy.wait_recv()
        at = red.at[p, mine]
        last.append(go(at, at, s_x.at[p], r_x.at[p], other_x))
    for copy in small:
        copy.wait_recv()
    pieces = [sbuf[2], srecv[3], srecv[4], srecv[5]]
    value = jnp.zeros(gs.shape, F32)
    for zi in range(4):
        back_by = lax.rem(z - zi + 4, 4)
        pick = pieces[0]
        for d in (1, 2, 3):
            pick = jnp.where(back_by == d, pieces[d], pick)
        value = value + pick
    sm_out[...] = value
    for copy in last:
        copy.wait_recv()
    for copy in started:
        copy.wait_send()


def layer(tokens, cotangent, lens, w_in, w_out, params):
    vmem = pl.BlockSpec(memory_space=pltpu.VMEM)
    shape = jax.ShapeDtypeStruct
    dma = pltpu.SemaphoreType.DMA
    return pl.pallas_call(
        layer_kernel,
        out_shape=(
            shape((T, D), BF), shape((T, D), BF), shape((PIECES, CH, PR, CW), BF), shape((8, CHAN), F32),
        ),
        in_specs=[vmem, vmem, pl.BlockSpec(memory_space=pltpu.SMEM)] + [vmem] * 3,
        out_specs=[vmem] * 4,
        scratch_shapes=[
            pltpu.VMEM((T, DI), F32), pltpu.VMEM((T, CHAN), F32), pltpu.VMEM((T, CHAN), F32),
            pltpu.VMEM((T, CHAN), BF), pltpu.VMEM((T, DI), F32), pltpu.VMEM((HEADS, T, T), F32),
            pltpu.VMEM((T, PADC), BF), pltpu.VMEM((D, 128), BF), pltpu.VMEM((4, 192, T), BF),
            pltpu.VMEM((4, 384, T), BF), pltpu.VMEM((T, DI), F32), pltpu.VMEM((T, D), BF),
            pltpu.VMEM((T, DI), F32), pltpu.VMEM((T, CHAN), F32),
            pltpu.VMEM((4, 384, D), BF), pltpu.VMEM((T, D), BF), pltpu.VMEM((3, T, D), BF),
            pltpu.VMEM((3, 192, T), BF), pltpu.VMEM((3, 384, T), BF), pltpu.VMEM((3, T, PADC), BF),
            pltpu.VMEM((PIECES, CH, PR, CW), BF), pltpu.VMEM((PIECES, 4, PR, CW), BF),
            pltpu.VMEM((PIECES, 3, PR, CW), BF), pltpu.VMEM((8, CHAN), F32),
            pltpu.VMEM((3, 8, CHAN), F32), pltpu.VMEM((6, 8, CHAN), F32),
            dma((5,)), dma((5,)), dma((3,)), dma((3,)), dma((3,)), dma((3,)), dma((3,)), dma((3,)),
            dma((2, 3)), dma((2, 3)), dma((PIECES,)), dma((PIECES,)), dma((PIECES, 3)), dma((PIECES, 3)),
            dma((PIECES, 3)), dma((PIECES, 3)), dma((PIECES,)), dma((PIECES,)), dma((6,)), dma((6,)),
        ],
        compiler_params=pltpu.CompilerParams(
            collective_id=1, has_side_effects=True, vmem_limit_bytes=VMEM_BYTES
        ),
        name="layer",
    )(tokens, cotangent, lens, w_in, w_out, params)


def adamw_kernel(red, wi, mi, vi, wo, mo, vo, nwi, nmi, nvi, nwo, nmo, nvo):
    def update(cols, grad, refs, rate, part=None):
        at = (slice(None), cols) if part is None else (part, slice(None), cols)
        gradient, master = grad.astype(F32), refs[0][at].astype(F32)
        first = beta_one * refs[1][at] + (1.0 - beta_one) * gradient
        second = beta_two * refs[2][at] + (1.0 - beta_two) * gradient * gradient
        root = jnp.sqrt(second * (1.0 / (1.0 - beta_two**STEP))) + adam_eps
        scale = rate / (1.0 - beta_one**STEP)
        new = (master * (1.0 - rate * 0.1) - scale * first / root, first, second)
        for ref, value in zip(refs[3:], new):
            ref[at] = value

    refs_in = (wi, mi, vi, nwi, nmi, nvi)
    refs_out = (wo, mo, vo, nwo, nmo, nvo)
    for k in range(5):
        update(slice(CW * k, CW * k + CW), red[0, k], refs_in, 0.05)
    update(slice(5 * CW, CIN), red[0, 5, :, :CIN - 5 * CW], refs_in, 0.05)
    update(slice(0, 384), red[0, 5, :, 256:], refs_out, 0.04, 0)
    update(slice(384, 768), red[0, 6, :, :384], refs_out, 0.04, 0)
    update(slice(0, 256), red[0, 6, :, 384:], refs_out, 0.04, 1)
    update(slice(256, 768), red[0, 7, :, :512], refs_out, 0.04, 1)


def adamw_all(red, w_in, m_in, v_in, w_out, m_out, v_out):
    rows = 16
    halves = [v.reshape(2, 192, D) for v in (w_out, m_out, v_out)]
    spec_in = pl.BlockSpec((rows, CIN), lambda i: (i, 0))
    spec_out = pl.BlockSpec((2, rows, D), lambda i: (0, i, 0))
    new = pl.pallas_call(
        adamw_kernel,
        grid=(192 // rows,),
        out_shape=[jax.ShapeDtypeStruct((192, CIN), F32)] * 3 + [jax.ShapeDtypeStruct((2, 192, D), F32)] * 3,
        in_specs=[pl.BlockSpec((1, CH, rows, CW), lambda i: (i // 3, 0, i % 3, 0))]
        + [spec_in] * 3 + [spec_out] * 3,
        out_specs=[spec_in] * 3 + [spec_out] * 3,
        compiler_params=pltpu.CompilerParams(vmem_limit_bytes=VMEM_BYTES),
        name="adamw",
    )(red, w_in, m_in, v_in, *halves)
    return list(new[:3]) + [v.reshape(384, D) for v in new[3:]]


def on_device_fast(
    tokens, cotangent, seq_lengths, w_in, w_out, w_small, m_in, v_in, m_out, v_out, m_small, v_small
):
    share = w_small.shape[0]
    small = jnp.pad(w_small, (0, 32 * 128 - share)).reshape(32, 128)
    full_in, full_small = gather_weights(w_in, small)
    packed = full_small.reshape(4, 32 * 128)[:, :share].reshape(4 * share).astype(F32)
    start = (KCONV + 1) * CHAN
    gains = start + 3 * HEADS
    heads = jnp.pad(packed[start:gains].reshape(3, HEADS), ((0, 0), (0, 128 - HEADS)))
    params = jnp.concatenate([
        packed[:start], packed[gains : gains + D], heads.reshape(-1), jnp.zeros(CHAN - D - 384, F32),
        packed[gains + D :], jnp.zeros(2 * CHAN - DI, F32),
    ]).reshape(8, CHAN)
    out, gx, red, sums = layer(
        tokens, cotangent, seq_lengths, full_in.reshape(D, CIN), w_out, params
    )
    flat = jnp.concatenate([
        sums[:5].reshape(-1), sums[5, D : D + HEADS], sums[5, D + 128 : D + 128 + HEADS],
        sums[5, D + 256 : D + 256 + HEADS], sums[5, :D], sums[6, :DI],
    ])
    share_small = lax.dynamic_slice_in_dim(flat, lax.axis_index("shard") * share, share)
    new = adamw_all(red, w_in, m_in, v_in, w_out, m_out, v_out)
    new_small = adamw(w_small, share_small, m_small, v_small, 0.3, 0.0)
    return (out, gx, *new, *new_small)


def solution(mesh):
    in_specs = (
        P(("replica", "shard"), None),
        P(("replica", "shard"), None),
        P(("replica", "shard"), None),
        P("shard", None),
        P("shard", None),
        P("shard"),
        P("shard", None),
        P("shard", None),
        P("shard", None),
        P("shard", None),
        P("shard"),
        P("shard"),
    )
    out_specs = (
        P(("replica", "shard"), None),
        P(("replica", "shard"), None),
        P("shard", None),
        P("shard", None),
        P("shard", None),
        P("shard", None),
        P("shard", None),
        P("shard", None),
        P("shard"),
        P("shard"),
        P("shard"),
    )
    fast = dict(mesh.shape) == {"replica": 8, "shard": 4}
    return jax.shard_map(
        on_device_fast if fast else on_device, mesh=mesh, in_specs=in_specs, out_specs=out_specs, check_vma=False
    )
```

```python
import jax
import jax.numpy as jnp
from jax import lax
from jax.experimental import pallas as pl
from jax.experimental.pallas import tpu as pltpu
from jax.sharding import PartitionSpec as P

D = 768
STATE = 128
HEAD = 64
KCONV = 4
STEP = 10
DI = 1536


epsilon = 1e-05
beta_one = 0.9
beta_two = 0.95
adam_eps = 1e-08


def make_rounders():

    def round_plain(value):
        return lax.optimization_barrier(value.astype(jnp.bfloat16)).astype(jnp.float32)

    def unchanged(value):
        return value

    round_value = jax.custom_vjp(round_plain)
    round_grad = jax.custom_vjp(unchanged)

    def value_keep(value):
        return (round_plain(value), None)

    def value_pass(kept, gradient):
        return (gradient,)

    def grad_keep(value):
        return (value, None)

    def grad_round(kept, gradient):
        return (round_plain(gradient),)

    round_value.defvjp(value_keep, value_pass)
    round_grad.defvjp(grad_keep, grad_round)
    return (round_value, round_grad)


def mixer(resid, weight_in, weight_out, packed, seglens, round_value, round_grad):
    rows_count = resid.shape[0]
    channels = DI + 2 * STATE
    heads = DI // HEAD
    kernel = packed[: KCONV * channels].reshape(KCONV, channels)
    conv_bias = packed[KCONV * channels : (KCONV + 1) * channels]
    start = (KCONV + 1) * channels
    step_bias = packed[start : start + heads]
    decay_log = packed[start + heads : start + 2 * heads]
    skip_gain = packed[start + 2 * heads : start + 3 * heads]
    pre_gain = packed[start + 3 * heads : start + 3 * heads + D]
    gate_gain = packed[start + 3 * heads + D :]
    places = jnp.arange(rows_count, dtype=jnp.int32)
    bounds = jnp.cumsum(seglens)
    segment = jnp.sum((places[:, None] >= bounds[None, :]).astype(jnp.int32), axis=1)
    meansq = jnp.mean(resid * resid, axis=1, keepdims=True)
    normed = resid * lax.rsqrt(meansq + epsilon) * pre_gain
    project = round_grad(
        jnp.dot(round_value(normed), weight_in, preferred_element_type=jnp.float32)
    )
    gate_raw = project[:, :DI]
    conv_in = project[:, DI : DI + channels]
    step_raw = project[:, DI + channels :]
    convolved = conv_bias + kernel[KCONV - 1] * conv_in
    for offset in range(1, KCONV):
        shifted = jnp.concatenate(
            [jnp.zeros((offset, channels), jnp.float32), conv_in[:-offset]], axis=0
        )
        earlier = jnp.concatenate([jnp.full((offset,), -1, jnp.int32), segment[:-offset]])
        within = (earlier == segment).astype(jnp.float32)[:, None]
        convolved = convolved + kernel[KCONV - 1 - offset] * shifted * within
    activated = jax.nn.silu(convolved)
    inner = round_value(activated[:, :DI])
    in_state = round_value(activated[:, DI : DI + STATE])
    out_state = round_value(activated[:, DI + STATE :])
    step_size = jax.nn.softplus(step_raw + step_bias)
    logrates = jnp.cumsum(step_size * -jnp.exp(decay_log), axis=0)
    intersection = round_grad(jnp.dot(out_state, in_state.T, preferred_element_type=jnp.float32))
    allowed = (segment[:, None] == segment[None, :]) & (places[:, None] >= places[None, :])
    group_count = heads // 8
    rates_grouped = logrates.reshape(rows_count, group_count, 8).transpose(1, 0, 2)
    steps_grouped = step_size.reshape(rows_count, group_count, 8).transpose(1, 0, 2)
    inner_grouped = inner.reshape(rows_count, group_count, 8, HEAD).transpose(1, 0, 2, 3)

    def mix_group(entry):
        rate_part, step_part, inner_part = entry
        spread = rate_part.T[:, :, None] - rate_part.T[:, None, :]
        weights = round_value(
            intersection[None]
            * jnp.exp(jnp.where(allowed[None], spread, -1e30))
            * step_part.T[:, None, :]
        )
        return jnp.einsum("hts,shp->thp", weights, inner_part, preferred_element_type=jnp.float32)

    mixed = lax.map(jax.checkpoint(mix_group), (rates_grouped, steps_grouped, inner_grouped))
    scanned = round_grad(mixed.transpose(1, 0, 2, 3).reshape(rows_count, DI)) + inner * jnp.repeat(
        skip_gain, HEAD
    )
    gated = scanned * jax.nn.silu(gate_raw)
    gatesq = jnp.mean(gated * gated, axis=1, keepdims=True)
    normed_two = gated * lax.rsqrt(gatesq + epsilon) * gate_gain
    output = round_grad(
        jnp.dot(round_value(normed_two), weight_out, preferred_element_type=jnp.float32)
    )
    return resid + output


def adamw(weight, gradient, first, second, rate, decay):
    first_new = beta_one * first + (1.0 - beta_one) * gradient
    second_new = beta_two * second + (1.0 - beta_two) * gradient * gradient
    corrected = (
        first_new
        / (1.0 - beta_one**STEP)
        / (jnp.sqrt(second_new / (1.0 - beta_two**STEP)) + adam_eps)
    )
    master = weight.astype(jnp.float32)
    return (master - rate * (corrected + decay * master), first_new, second_new)


def reduce_group(grads):
    shares = (
        lax.psum_scatter(grads[0], "shard", scatter_dimension=0, tiled=True),
        lax.psum_scatter(grads[1], "shard", scatter_dimension=0, tiled=True),
        lax.psum_scatter(grads[2], "shard", scatter_dimension=0, tiled=True),
    )
    return lax.psum((shares[0], shares[1], shares[2]), "replica")


def on_device(
    tokens, cotangent, seq_lengths, w_in, w_out, w_small, m_in, v_in, m_out, v_out, m_small, v_small
):
    round_value, round_grad = make_rounders()
    full_in, full_out, full_small = (
        lax.all_gather(w_in, "shard", axis=0, tiled=True),
        lax.all_gather(w_out, "shard", axis=0, tiled=True),
        lax.all_gather(w_small, "shard", axis=0, tiled=True),
    )
    seglens = seq_lengths[0]

    def local(resid, weight_in, weight_out, packed):
        return mixer(resid, weight_in, weight_out, packed, seglens, round_value, round_grad)

    result, pullback = jax.vjp(
        local,
        tokens.astype(jnp.float32),
        full_in.astype(jnp.float32),
        full_out.astype(jnp.float32),
        full_small.astype(jnp.float32),
    )
    places = jnp.arange(tokens.shape[0], dtype=jnp.int32)
    valid = (places < tokens.shape[0] - seglens[-1]).astype(jnp.float32)[:, None]
    grad_x, grad_in, grad_out, grad_small = pullback(cotangent.astype(jnp.float32) * valid)
    share_in, share_out, share_small = reduce_group((grad_in, grad_out, grad_small))
    new_w_in, new_m_in, new_v_in = adamw(w_in, share_in, m_in, v_in, 0.05, 0.1)
    new_w_out, new_m_out, new_v_out = adamw(w_out, share_out, m_out, v_out, 0.04, 0.1)
    new_w_small, new_m_small, new_v_small = adamw(w_small, share_small, m_small, v_small, 0.3, 0.0)
    return (
        result.astype(jnp.bfloat16),
        grad_x.astype(jnp.bfloat16),
        new_w_in,
        new_m_in,
        new_v_in,
        new_w_out,
        new_m_out,
        new_v_out,
        new_w_small,
        new_m_small,
        new_v_small,
    )


CHAN = DI + 2 * STATE
HEADS = DI // HEAD
CIN = DI + CHAN + HEADS
MAIN = DI + CHAN
PADC = MAIN + 128
T = 128
PIECES = 4
PR = 48
CH = 8
CW = 640
SROWS = 24
MESH = pl.DeviceIdType.MESH
VMEM_BYTES = 24 * 1024 * 1024
LAYER_BYTES = 40 * 1024 * 1024
BF = jnp.bfloat16
F32 = jnp.float32


def place():
    replica, shard = lax.axis_index("replica"), lax.axis_index("shard")
    return replica // 2, replica % 2, shard // 2, shard % 2


def target(z, x, y, c):
    return (z * 2 + x, y * 2 + c)


def greet(peers):
    barrier = pltpu.get_barrier_semaphore()
    for peer in peers:
        pl.semaphore_signal(barrier, inc=1, device_id=peer, device_id_type=MESH)
    pl.semaphore_wait(barrier, len(peers))


def send(src, dst, send_sem, recv_sem, peer):
    copy = pltpu.make_async_remote_copy(
        src_ref=src, dst_ref=dst, send_sem=send_sem, recv_sem=recv_sem,
        device_id=peer, device_id_type=MESH,
    )
    copy.start()
    return copy


def gather_kernel(wi, sm, fi, fs, loc, s_own, r_own, s_y, r_y, s_x, r_x, s_sm, r_sm):
    z, x, y, c = place()
    core, other_y = target(z, x, y, 1 - c), target(z, x, 1 - y, c)
    diag, other_x = target(z, x, 1 - y, 1 - c), target(z, 1 - x, y, c)
    greet((core, other_y, diag, other_x))
    me = 2 * y + c
    far = (2 * (1 - y) + c, 2 * (1 - y) + 1 - c)
    small = [
        send(sm, fs.at[me], s_sm.at[i], r_sm.at[i], peer) for i, peer in enumerate((core, other_y, diag))
    ]
    over_y = []
    for u in range(GATHER):
        here = pl.ds(pl.multiple_of(x * 96 + 96 // GATHER * u, 16), 96 // GATHER)
        over_y.append([
            send(wi.at[here], fi.at[me, here], s_y.at[u, i], r_y.at[u, i], peer)
            for i, peer in enumerate((other_y, diag))
        ])
    own = send(wi, fi.at[me], s_own.at[0], r_own.at[0], core)
    keep = [
        pltpu.make_async_copy(src, full.at[me], loc.at[i])
        for i, (src, full) in enumerate(((wi, fi), (sm, fs)))
    ]
    for copy in keep:
        copy.start()
    over_x = []
    for u in range(GATHER):
        here = pl.ds(pl.multiple_of(x * 96 + 96 // GATHER * u, 16), 96 // GATHER)
        for i in range(2):
            over_y[u][i].wait_recv()
            part = fi.at[far[i], here]
            over_x.append(send(part, part, s_x.at[u, i], r_x.at[u, i], other_x))
    for copy in keep:
        copy.wait()
    for copy in small + [own] + over_x:
        copy.wait_recv()
    for copy in small + [own] + over_x + [copy for pair in over_y for copy in pair]:
        copy.wait_send()


GATHER = 3


def gather_weights(w_in, small):
    dma = pltpu.SemaphoreType.DMA
    return pl.pallas_call(
        gather_kernel,
        out_shape=(
            jax.ShapeDtypeStruct((4, 192, CIN), BF),
            jax.ShapeDtypeStruct((4, 32, 128), BF),
        ),
        in_specs=[pl.BlockSpec(memory_space=pl.ANY)] * 2,
        out_specs=[pl.BlockSpec(memory_space=pl.ANY)] * 2,
        scratch_shapes=[dma((2,)), dma((1,)), dma((1,)), dma((GATHER, 2)), dma((GATHER, 2)),
                        dma((GATHER, 2)), dma((GATHER, 2)), dma((3,)), dma((3,))],
        compiler_params=pltpu.CompilerParams(collective_id=0, has_side_effects=True),
        name="gather_weights",
    )(w_in, small)


def dot(a, b):
    return jnp.dot(a, b, preferred_element_type=F32)


def dot_nt(a, b):
    return lax.dot_general(a, b, (((1,), (1,)), ((), ())), preferred_element_type=F32)


def dot_tn(a, b):
    return lax.dot_general(a, b, (((0,), (0,)), ((), ())), preferred_element_type=F32)


def colsum(v):
    return jnp.sum(v, axis=0, keepdims=True)


def layer_kernel(
    x_ref, ct_ref, len_ref, wi_ref, wo_own, par_ref,
    out_ref, gx_ref, red, sm_out,
    gate, ci, conv, inner, scan, mixes, dproj, tail, nt, n2t, gated, n16, dact,
    dn2_all, dn2_out, out_part, out_in, d_own, d_in, n_in, n2_in, dp_in, own, half_in, rz, gs, sbuf, srecv,
    s_o, r_o, s_w, r_w, s_d, r_d, s_n, r_n, s_2, r_2, s_p, r_p, s_h, r_h, s_z, r_z, s_g, r_g, s_x, r_x, s_s, r_s,
):
    z, x_at, y, c = place()
    core, other_y = target(z, x_at, y, 1 - c), target(z, x_at, 1 - y, c)
    diag, other_x = target(z, x_at, 1 - y, 1 - c), target(z, 1 - x_at, y, c)
    others = [lax.rem(z + d, 4) for d in (1, 2, 3)]
    over_z = [target(o, x_at, y, c) for o in others]
    greet([core, other_y, diag, other_x] + over_z)
    started = []

    def go(*args):
        copy = send(*args)
        started.append(copy)
        return copy

    me, far = 2 * y + c, 2 * (1 - y) + c
    group = [(core, 2 * y + 1 - c), (other_y, far), (diag, 2 * (1 - y) + 1 - c)]
    taps_ref, cb_ref = par_ref.at[0:4], par_ref.at[4:5]
    pg_ref, gg_ref = par_ref.at[5:6, 0:D], par_ref.at[6:7, 0:DI]
    step_bias, decay_log, skips = (par_ref[5:6, 768 + 128 * i:896 + 128 * i] for i in range(3))
    gs[...] = jnp.zeros(gs.shape, F32)
    bounds = [len_ref[0, 0]]
    for i in range(1, 4):
        bounds.append(bounds[-1] + len_ref[0, i])
    row = lax.broadcasted_iota(jnp.int32, (T, 1), 0)
    lane = lax.broadcasted_iota(jnp.int32, (1, T), 1)

    def segment(places):
        total = jnp.zeros(places.shape, jnp.int32)
        for bound in bounds:
            total = total + (places >= bound).astype(jnp.int32)
        return total

    seg_row, seg_lane = segment(row), segment(lane)
    within = [None] + [
        ((row >= j) & (segment(row - j) == seg_row)).astype(F32) for j in range(1, KCONV)
    ]
    allowed = (seg_row == seg_lane) & (row >= lane)
    valid = (row < bounds[2]).astype(F32)

    x = x_ref[...].astype(F32)
    r1 = lax.rsqrt(jnp.mean(x * x, axis=1, keepdims=True) + epsilon)
    normed = x * r1 * pg_ref[...]
    n16[...] = normed.astype(BF)
    nt[...] = normed.T.astype(BF).reshape(4, 192, T)
    dy = ct_ref[...].astype(F32) * valid
    d16 = dy.astype(BF)
    d_own[...] = d16
    d_got, n_got, n2_got = [], [], []
    for i, (peer, shard) in enumerate(group):
        d_got.append(go(d_own, d_in.at[i], s_d.at[i], r_d.at[i], peer))
    for i, (peer, shard) in enumerate(group):
        n_got.append(go(nt.at[shard], n_in.at[i], s_n.at[i], r_n.at[i], peer))
    dn2_all[me] = dot_nt(d16, wo_own[...]).astype(BF)
    tail[...] = jnp.zeros(tail.shape, BF)
    tail[:, :HEADS] = wi_ref[:, MAIN:]
    n = n16[...]
    step_in = dot(n, tail[...]) + step_bias
    for k in range(0, DI, 512):
        gate[:, k:k + 512] = dot(n, wi_ref[:, k:k + 512])
    W = 256
    for k in range(0, CHAN, W):
        cols = slice(k, k + W)
        v = dot(n, wi_ref[:, DI + k:DI + k + W])
        ci[:, cols] = v
        total = cb_ref[:, cols] + taps_ref[KCONV - 1:KCONV, cols] * v
        for j in range(1, KCONV):
            total = total + taps_ref[KCONV - 1 - j:KCONV - j, cols] * pltpu.roll(v, j, 0) * within[j]
        conv[:, cols] = total
        inner[:, cols] = (total * jax.nn.sigmoid(total)).astype(BF)
    dn2_got = []
    for i, (peer, shard) in enumerate(group):
        d_got[i].wait_recv()
        dn2_out[i] = dot_nt(d_in[i], wo_own[...]).astype(BF)
        dn2_got.append(go(dn2_out.at[i], dn2_all.at[me], s_w.at[i], r_w.at[i], peer))
    step = jnp.maximum(step_in, 0.0) + jnp.log1p(jnp.exp(-jnp.abs(step_in)))
    rate = -jnp.exp(decay_log)
    tri = (row >= lane).astype(F32)
    logs = jnp.dot(tri, step * rate, precision=lax.Precision.HIGHEST, preferred_element_type=F32)
    logs_t, step_t = logs.T, step.T
    in_state, out_state = inner[:, DI:DI + STATE], inner[:, DI + STATE:]
    inter = dot_nt(out_state, in_state)
    left = lane < HEAD

    def skip_of(q):
        return jnp.where(left, skips[:, 2 * q:2 * q + 1], skips[:, 2 * q + 1:2 * q + 2])

    gsq = jnp.zeros((T, 1), F32)
    for q in range(HEADS // 2):
        cols = slice(128 * q, 128 * q + 128)
        pair = inner[:, cols]
        parts = []
        for h in (2 * q, 2 * q + 1):
            spread = logs[:, h:h + 1] - logs_t[h:h + 1, :]
            decay = jnp.exp(jnp.where(allowed, spread, -1e30))
            mixes[h] = decay
            parts.append(dot((inter * decay * step_t[h:h + 1, :]).astype(BF), pair))
        value = jnp.where(left, parts[0], parts[1]) + pair.astype(F32) * skip_of(q)
        scan[:, cols] = value
        g = gate[:, cols]
        value = value * (g * jax.nn.sigmoid(g))
        gated[:, cols] = value
        gsq = gsq + jnp.sum(value * value, axis=1, keepdims=True)
    r2 = lax.rsqrt(gsq * (1.0 / DI) + epsilon)

    for k in range(0, DI, 128):
        n2t[k // 384, k % 384:k % 384 + 128, :] = (
            gated[:, k:k + 128] * r2 * gg_ref[:, k:k + 128]
        ).T.astype(BF)
    for i, (peer, shard) in enumerate(group):
        n2_got.append(go(n2t.at[shard], n2_in.at[i], s_2.at[i], r_2.at[i], peer))
    for copy in dn2_got:
        copy.wait_recv()
    mean_ug = jnp.zeros((T, 1), F32)
    W = 128
    for k in range(0, DI, W):
        cols = slice(k, k + W)
        g = gated[:, cols]
        dn2 = dn2_all[k // 384, :, k % 384:k % 384 + W].astype(F32)
        gs[6:7, cols] = colsum(dn2 * (g * r2))
        mean_ug = mean_ug + jnp.sum(dn2 * gg_ref[:, cols] * g, axis=1, keepdims=True)
    back = mean_ug * (1.0 / DI) * r2 * r2

    dinter = jnp.zeros((T, T), F32)
    dlog = jnp.zeros((T, T), F32)
    dskip = jnp.zeros((1, T), F32)
    dstep_rows, dlog_rows = [], []
    for q in range(HEADS // 2):
        cols = slice(128 * q, 128 * q + 128)
        g, value, gt = gate[:, cols], scan[:, cols], gated[:, cols]
        dgated = r2 * (dn2_all[q // 3, :, 128 * (q % 3):128 * (q % 3) + 128].astype(F32) * gg_ref[:, cols] - gt * back)
        sig = jax.nn.sigmoid(g)
        dscan = dgated * (g * sig)
        dproj[:, cols] = (dgated * value * (sig * (1.0 + g * (1.0 - sig)))).astype(BF)
        pair = inner[:, cols]
        pair32 = pair.astype(F32)
        by_lane = colsum(dscan * pair32)
        ds16 = dscan.astype(BF)
        parts = []
        for side, h in enumerate((2 * q, 2 * q + 1)):
            decay, srow = mixes[h], step_t[h:h + 1, :]
            mine = jnp.where(left if side == 0 else jnp.logical_not(left), pair32, 0.0).astype(BF)
            dmix = dot_nt(ds16, mine) * decay
            half = jnp.where(left if side == 0 else jnp.logical_not(left), by_lane, 0.0)
            dskip = dskip + jnp.where(lane == h, jnp.sum(half, axis=1, keepdims=True), 0.0)
            dinter = dinter + dmix * srow
            wide = dmix * inter
            per_source = colsum(wide)
            dstep_rows.append(per_source)
            dlog_rows.append(-per_source * srow)
            dlog = dlog + jnp.where(lane == h, jnp.sum(wide * srow, axis=1, keepdims=True), 0.0)
            parts.append(dot_tn((inter * decay * srow).astype(BF), ds16))
        dact[:, cols] = jnp.where(left, parts[0], parts[1]) + dscan * skip_of(q)
    def spread_dproj(part, cols):
        return [
            go(dproj.at[:, cols], dp_in.at[i, :, cols], s_p.at[part, i], r_p.at[part, i], group[i][0])
            for i in range(2)
        ]

    dp_got = [spread_dproj(0, pl.ds(0, DI))]
    out_got = []
    for i, (peer, shard) in enumerate(group):
        n2_got[i].wait_recv()
        out_part[i] = dot_tn(n2_in[i], wo_own[...]).astype(BF)
        out_got.append(go(out_part.at[i], out_in.at[i], s_o.at[i], r_o.at[i], peer))
    rest = jnp.zeros((T - HEADS, T), F32)
    dstep = jnp.concatenate(dstep_rows + [rest], axis=0).T
    dlog = dlog + jnp.concatenate(dlog_rows + [rest], axis=0).T
    di16 = dinter.astype(BF)
    dact[:, DI:DI + STATE] = dot_tn(di16, out_state)
    dact[:, DI + STATE:] = dot(di16, in_state)
    upper = (row <= lane).astype(F32)
    ddecay = jnp.dot(upper, dlog, precision=lax.Precision.HIGHEST, preferred_element_type=F32)
    dstep = dstep + ddecay * rate
    draw = dstep * jax.nn.sigmoid(step_in)
    gs[5:6, 768:896] = colsum(draw)
    gs[5:6, 896:1024] = colsum(ddecay * step * rate)
    gs[5:6, 1024:1152] = dskip
    dproj[:, MAIN:] = draw.astype(BF)
    W = 256
    for k in range(0, CHAN, W):
        cols = slice(k, k + W)
        v, raw = conv[:, cols], ci[:, cols]
        sig = jax.nn.sigmoid(v)
        dconv = dact[:, cols] * (sig * (1.0 + v * (1.0 - sig)))
        gs[4:5, cols] = colsum(dconv)
        gs[KCONV - 1:KCONV, cols] = colsum(dconv * raw)
        dci = dconv * taps_ref[KCONV - 1:KCONV, cols]
        for j in range(1, KCONV):
            here = dconv * within[j]
            gs[KCONV - 1 - j:KCONV - j, cols] = colsum(here * pltpu.roll(raw, j, 0))
            dci = dci + pltpu.roll(here * taps_ref[KCONV - 1 - j:KCONV - j, cols], T - j, 0)
        dproj[:, DI + k:DI + k + W] = dci.astype(BF)

    dp_got.append(spread_dproj(1, pl.ds(DI, PADC - DI)))
    dn = dot_nt(dproj[:, MAIN:], tail[...])
    for k in range(0, MAIN, 256):
        dn = dn + dot_nt(dproj[:, k:k + 256], wi_ref[:, k:k + 256])
    xr = x * r1
    gs[5:6, 0:D] = colsum(dn * xr)
    u = dn * pg_ref[...]
    dx = r1 * (u - xr * jnp.mean(u * xr, axis=1, keepdims=True)) + dy
    gx_ref[...] = dx.astype(BF)

    small_copy = go(gs, srecv.at[0], s_s.at[0], r_s.at[0], core)
    forwarded = []
    for part, cols in enumerate((pl.ds(0, DI), pl.ds(DI, PADC - DI))):
        dp_got[part][1].wait_recv()
        forwarded.append(go(
            dp_in.at[1, :, cols], dp_in.at[2, :, cols], s_p.at[part, 2], r_p.at[part, 2], core
        ))
        dp_got[part][0].wait_recv()
    for copy in n_got:
        copy.wait_recv()
    n_all = [nt[me]] + [n_in[i] for i in range(3)]
    n2_all = [n2t[me]] + [n2_in[i] for i in range(3)]
    d_all = [d_own] + [d_in.at[i] for i in range(3)]
    dp_all = [dproj] + [dp_in.at[i] for i in range(3)]

    def put(chunk, first, value):
        wide = value.shape[1]
        own[:, chunk, :, first:first + wide] = value.astype(BF).reshape(PIECES, PR, wide)

    def total(lefts, rights, cols):
        value = dot(lefts[0], rights[0][:, cols])
        for a, b in zip(lefts[1:], rights[1:]):
            value = value + dot(a, b[:, cols])
        return value

    rows_a, rows_b = [v[:192] for v in n2_all], [v[192:] for v in n2_all]
    put(5, 256, total(rows_a, d_all, slice(0, 384)))
    put(6, 0, total(rows_a, d_all, slice(384, 768)))
    put(6, 384, total(rows_b, d_all, slice(0, 256)))
    put(7, 0, total(rows_b, d_all, slice(256, 768)))
    put(7, 512, jnp.zeros((192, 128), F32))
    small_copy.wait_recv()
    sbuf[0] = gs[...] + srecv[0]
    small_copy = go(sbuf.at[0], srecv.at[1], s_s.at[1], r_s.at[1], other_y)
    forwarded[0].wait_recv()
    for k in range(2):
        put(k, 0, total(n_all, dp_all, slice(CW * k, CW * k + CW)))
    forwarded[1].wait_recv()
    for k in range(2, 5):
        put(k, 0, total(n_all, dp_all, slice(CW * k, CW * k + CW)))
    put(5, 0, total(n_all, dp_all, slice(5 * CW, PADC)))

    mine, away = pl.ds(4 * x_at, 4), pl.ds(4 * (1 - x_at), 4)
    halves = [go(own.at[p, away], half_in.at[p], s_h.at[p], r_h.at[p], other_x) for p in range(PIECES)]
    small_copy.wait_recv()
    sbuf[1] = sbuf[0] + srecv[1]
    small_copy = go(sbuf.at[1], srecv.at[2], s_s.at[2], r_s.at[2], other_x)
    spread = []
    for p in range(PIECES):
        halves[p].wait_recv()
        for i in range(4):
            at = own.at[p, 4 * x_at + i]
            at[...] = (at[...].astype(F32) + half_in[p, i].astype(F32)).astype(BF)
        spread.append([
            go(own.at[p, 4 * x_at + others[d]], rz.at[p, d], s_z.at[p, d], r_z.at[p, d], over_z[d])
            for d in range(3)
        ])
    small_copy.wait_recv()
    sbuf[2] = sbuf[1] + srecv[2]
    small = [go(sbuf.at[2], srecv.at[3 + d], s_s.at[3 + d], r_s.at[3 + d], over_z[d]) for d in range(3)]
    back = []
    for p in range(PIECES):
        for copy in spread[p]:
            copy.wait_recv()
        value = own[p, 4 * x_at + z].astype(F32)
        for d in range(3):
            value = value + rz[p, d].astype(F32)
        at = red.at[p, 4 * x_at + z]
        at[...] = value.astype(BF)
        back.append([go(at, at, s_g.at[p, d], r_g.at[p, d], over_z[d]) for d in range(3)])
    last = []
    for p in range(PIECES):
        for copy in back[p]:
            copy.wait_recv()
        at = red.at[p, mine]
        last.append(go(at, at, s_x.at[p], r_x.at[p], other_x))
    for copy in small:
        copy.wait_recv()
    pieces = [sbuf[2], srecv[3], srecv[4], srecv[5]]
    value = jnp.zeros(gs.shape, F32)
    for zi in range(4):
        back_by = lax.rem(z - zi + 4, 4)
        pick = pieces[0]
        for d in (1, 2, 3):
            pick = jnp.where(back_by == d, pieces[d], pick)
        value = value + pick
    sm_out[...] = value
    out = x_ref[...].astype(F32) + dot_tn(n2t[me], wo_own[...])
    for i in range(3):
        out_got[i].wait_recv()
        out = out + out_in[i].astype(F32)
    out_ref[...] = out.astype(BF)
    for copy in last:
        copy.wait_recv()
    for copy in started:
        copy.wait_send()


def layer(tokens, cotangent, lens, w_in, w_out, params):
    vmem = pl.BlockSpec(memory_space=pltpu.VMEM)
    shape = jax.ShapeDtypeStruct
    dma = pltpu.SemaphoreType.DMA
    return pl.pallas_call(
        layer_kernel,
        out_shape=(
            shape((T, D), BF), shape((T, D), BF), shape((PIECES, CH, PR, CW), BF), shape((8, CHAN), F32),
        ),
        in_specs=[vmem, vmem, pl.BlockSpec(memory_space=pltpu.SMEM)] + [vmem] * 3,
        out_specs=[vmem] * 4,
        scratch_shapes=[
            pltpu.VMEM((T, DI), F32), pltpu.VMEM((T, CHAN), F32), pltpu.VMEM((T, CHAN), F32),
            pltpu.VMEM((T, CHAN), BF), pltpu.VMEM((T, DI), F32), pltpu.VMEM((HEADS, T, T), F32),
            pltpu.VMEM((T, PADC), BF), pltpu.VMEM((D, 128), BF), pltpu.VMEM((4, 192, T), BF),
            pltpu.VMEM((4, 384, T), BF), pltpu.VMEM((T, DI), F32), pltpu.VMEM((T, D), BF),
            pltpu.VMEM((T, CHAN), F32),
            pltpu.VMEM((4, T, 384), BF), pltpu.VMEM((3, T, 384), BF), pltpu.VMEM((3, T, D), BF),
            pltpu.VMEM((3, T, D), BF), pltpu.VMEM((T, D), BF), pltpu.VMEM((3, T, D), BF),
            pltpu.VMEM((3, 192, T), BF), pltpu.VMEM((3, 384, T), BF), pltpu.VMEM((3, T, PADC), BF),
            pltpu.VMEM((PIECES, CH, PR, CW), BF), pltpu.VMEM((PIECES, 4, PR, CW), BF),
            pltpu.VMEM((PIECES, 3, PR, CW), BF), pltpu.VMEM((8, CHAN), F32),
            pltpu.VMEM((3, 8, CHAN), F32), pltpu.VMEM((6, 8, CHAN), F32),
            dma((3,)), dma((3,)), dma((3,)), dma((3,)), dma((3,)), dma((3,)), dma((3,)), dma((3,)), dma((3,)), dma((3,)),
            dma((2, 3)), dma((2, 3)), dma((PIECES,)), dma((PIECES,)), dma((PIECES, 3)), dma((PIECES, 3)),
            dma((PIECES, 3)), dma((PIECES, 3)), dma((PIECES,)), dma((PIECES,)), dma((6,)), dma((6,)),
        ],
        compiler_params=pltpu.CompilerParams(
            collective_id=1, has_side_effects=True, vmem_limit_bytes=LAYER_BYTES
        ),
        name="layer",
    )(tokens, cotangent, lens, w_in, w_out, params)


def adamw_kernel(red, wi, mi, vi, wo, mo, vo, nwi, nmi, nvi, nwo, nmo, nvo):
    def update(cols, grad, refs, rate, part=None):
        at = (slice(None), cols) if part is None else (part, slice(None), cols)
        gradient, master = grad.astype(F32), refs[0][at].astype(F32)
        first = beta_one * refs[1][at] + (1.0 - beta_one) * gradient
        second = beta_two * refs[2][at] + (1.0 - beta_two) * gradient * gradient
        root = jnp.sqrt(second * (1.0 / (1.0 - beta_two**STEP))) + adam_eps
        scale = rate / (1.0 - beta_one**STEP)
        new = (master * (1.0 - rate * 0.1) - scale * first / root, first, second)
        for ref, value in zip(refs[3:], new):
            ref[at] = value

    refs_in = (wi, mi, vi, nwi, nmi, nvi)
    refs_out = (wo, mo, vo, nwo, nmo, nvo)
    for k in range(5):
        update(slice(CW * k, CW * k + CW), red[0, k], refs_in, 0.05)
    update(slice(5 * CW, CIN), red[0, 5, :, :CIN - 5 * CW], refs_in, 0.05)
    update(slice(0, 384), red[0, 5, :, 256:], refs_out, 0.04, 0)
    update(slice(384, 768), red[0, 6, :, :384], refs_out, 0.04, 0)
    update(slice(0, 256), red[0, 6, :, 384:], refs_out, 0.04, 1)
    update(slice(256, 768), red[0, 7, :, :512], refs_out, 0.04, 1)


def adamw_all(red, w_in, m_in, v_in, w_out, m_out, v_out):
    rows = PR
    halves = [v.reshape(2, 192, D) for v in (w_out, m_out, v_out)]
    spec_in = pl.BlockSpec((rows, CIN), lambda i: (i, 0))
    spec_out = pl.BlockSpec((2, rows, D), lambda i: (0, i, 0))
    new = pl.pallas_call(
        adamw_kernel,
        grid=(192 // rows,),
        out_shape=[jax.ShapeDtypeStruct((192, CIN), F32)] * 3 + [jax.ShapeDtypeStruct((2, 192, D), F32)] * 3,
        in_specs=[pl.BlockSpec((1, CH, rows, CW), lambda i: (i, 0, 0, 0))]
        + [spec_in] * 3 + [spec_out] * 3,
        out_specs=[spec_in] * 3 + [spec_out] * 3,
        compiler_params=pltpu.CompilerParams(vmem_limit_bytes=VMEM_BYTES),
        name="adamw",
    )(red, w_in, m_in, v_in, *halves)
    return list(new[:3]) + [v.reshape(384, D) for v in new[3:]]


def on_device_fast(
    tokens, cotangent, seq_lengths, w_in, w_out, w_small, m_in, v_in, m_out, v_out, m_small, v_small
):
    share = w_small.shape[0]
    small = jnp.pad(w_small, (0, 32 * 128 - share)).reshape(32, 128)
    full_in, full_small = gather_weights(w_in, small)
    packed = full_small.reshape(4, 32 * 128)[:, :share].reshape(4 * share).astype(F32)
    start = (KCONV + 1) * CHAN
    gains = start + 3 * HEADS
    heads = jnp.pad(packed[start:gains].reshape(3, HEADS), ((0, 0), (0, 128 - HEADS)))
    params = jnp.concatenate([
        packed[:start], packed[gains : gains + D], heads.reshape(-1), jnp.zeros(CHAN - D - 384, F32),
        packed[gains + D :], jnp.zeros(2 * CHAN - DI, F32),
    ]).reshape(8, CHAN)
    out, gx, red, sums = layer(
        tokens, cotangent, seq_lengths, full_in.reshape(D, CIN), w_out, params
    )
    flat = jnp.concatenate([
        sums[:5].reshape(-1), sums[5, D : D + HEADS], sums[5, D + 128 : D + 128 + HEADS],
        sums[5, D + 256 : D + 256 + HEADS], sums[5, :D], sums[6, :DI],
    ])
    share_small = lax.dynamic_slice_in_dim(flat, lax.axis_index("shard") * share, share)
    new = adamw_all(red, w_in, m_in, v_in, w_out, m_out, v_out)
    new_small = adamw(w_small, share_small, m_small, v_small, 0.3, 0.0)
    return (out, gx, *new, *new_small)


def solution(mesh):
    in_specs = (
        P(("replica", "shard"), None),
        P(("replica", "shard"), None),
        P(("replica", "shard"), None),
        P("shard", None),
        P("shard", None),
        P("shard"),
        P("shard", None),
        P("shard", None),
        P("shard", None),
        P("shard", None),
        P("shard"),
        P("shard"),
    )
    out_specs = (
        P(("replica", "shard"), None),
        P(("replica", "shard"), None),
        P("shard", None),
        P("shard", None),
        P("shard", None),
        P("shard", None),
        P("shard", None),
        P("shard", None),
        P("shard"),
        P("shard"),
        P("shard"),
    )
    fast = dict(mesh.shape) == {"replica": 8, "shard": 4}
    return jax.shard_map(
        on_device_fast if fast else on_device, mesh=mesh, in_specs=in_specs, out_specs=out_specs, check_vma=False
    )
```

```python
import jax
import jax.numpy as jnp
from jax import lax
from jax.experimental import pallas as pl
from jax.experimental.pallas import tpu as pltpu
from jax.sharding import PartitionSpec as P

D = 768
STATE = 128
HEAD = 64
KCONV = 4
STEP = 10
DI = 1536


epsilon = 1e-05
beta_one = 0.9
beta_two = 0.95
adam_eps = 1e-08


def make_rounders():

    def round_plain(value):
        return lax.optimization_barrier(value.astype(jnp.bfloat16)).astype(jnp.float32)

    def unchanged(value):
        return value

    round_value = jax.custom_vjp(round_plain)
    round_grad = jax.custom_vjp(unchanged)

    def value_keep(value):
        return (round_plain(value), None)

    def value_pass(kept, gradient):
        return (gradient,)

    def grad_keep(value):
        return (value, None)

    def grad_round(kept, gradient):
        return (round_plain(gradient),)

    round_value.defvjp(value_keep, value_pass)
    round_grad.defvjp(grad_keep, grad_round)
    return (round_value, round_grad)


def mixer(resid, weight_in, weight_out, packed, seglens, round_value, round_grad):
    rows_count = resid.shape[0]
    channels = DI + 2 * STATE
    heads = DI // HEAD
    kernel = packed[: KCONV * channels].reshape(KCONV, channels)
    conv_bias = packed[KCONV * channels : (KCONV + 1) * channels]
    start = (KCONV + 1) * channels
    step_bias = packed[start : start + heads]
    decay_log = packed[start + heads : start + 2 * heads]
    skip_gain = packed[start + 2 * heads : start + 3 * heads]
    pre_gain = packed[start + 3 * heads : start + 3 * heads + D]
    gate_gain = packed[start + 3 * heads + D :]
    places = jnp.arange(rows_count, dtype=jnp.int32)
    bounds = jnp.cumsum(seglens)
    segment = jnp.sum((places[:, None] >= bounds[None, :]).astype(jnp.int32), axis=1)
    meansq = jnp.mean(resid * resid, axis=1, keepdims=True)
    normed = resid * lax.rsqrt(meansq + epsilon) * pre_gain
    project = round_grad(
        jnp.dot(round_value(normed), weight_in, preferred_element_type=jnp.float32)
    )
    gate_raw = project[:, :DI]
    conv_in = project[:, DI : DI + channels]
    step_raw = project[:, DI + channels :]
    convolved = conv_bias + kernel[KCONV - 1] * conv_in
    for offset in range(1, KCONV):
        shifted = jnp.concatenate(
            [jnp.zeros((offset, channels), jnp.float32), conv_in[:-offset]], axis=0
        )
        earlier = jnp.concatenate([jnp.full((offset,), -1, jnp.int32), segment[:-offset]])
        within = (earlier == segment).astype(jnp.float32)[:, None]
        convolved = convolved + kernel[KCONV - 1 - offset] * shifted * within
    activated = jax.nn.silu(convolved)
    inner = round_value(activated[:, :DI])
    in_state = round_value(activated[:, DI : DI + STATE])
    out_state = round_value(activated[:, DI + STATE :])
    step_size = jax.nn.softplus(step_raw + step_bias)
    logrates = jnp.cumsum(step_size * -jnp.exp(decay_log), axis=0)
    intersection = round_grad(jnp.dot(out_state, in_state.T, preferred_element_type=jnp.float32))
    allowed = (segment[:, None] == segment[None, :]) & (places[:, None] >= places[None, :])
    group_count = heads // 8
    rates_grouped = logrates.reshape(rows_count, group_count, 8).transpose(1, 0, 2)
    steps_grouped = step_size.reshape(rows_count, group_count, 8).transpose(1, 0, 2)
    inner_grouped = inner.reshape(rows_count, group_count, 8, HEAD).transpose(1, 0, 2, 3)

    def mix_group(entry):
        rate_part, step_part, inner_part = entry
        spread = rate_part.T[:, :, None] - rate_part.T[:, None, :]
        weights = round_value(
            intersection[None]
            * jnp.exp(jnp.where(allowed[None], spread, -1e30))
            * step_part.T[:, None, :]
        )
        return jnp.einsum("hts,shp->thp", weights, inner_part, preferred_element_type=jnp.float32)

    mixed = lax.map(jax.checkpoint(mix_group), (rates_grouped, steps_grouped, inner_grouped))
    scanned = round_grad(mixed.transpose(1, 0, 2, 3).reshape(rows_count, DI)) + inner * jnp.repeat(
        skip_gain, HEAD
    )
    gated = scanned * jax.nn.silu(gate_raw)
    gatesq = jnp.mean(gated * gated, axis=1, keepdims=True)
    normed_two = gated * lax.rsqrt(gatesq + epsilon) * gate_gain
    output = round_grad(
        jnp.dot(round_value(normed_two), weight_out, preferred_element_type=jnp.float32)
    )
    return resid + output


def adamw(weight, gradient, first, second, rate, decay):
    first_new = beta_one * first + (1.0 - beta_one) * gradient
    second_new = beta_two * second + (1.0 - beta_two) * gradient * gradient
    corrected = (
        first_new
        / (1.0 - beta_one**STEP)
        / (jnp.sqrt(second_new / (1.0 - beta_two**STEP)) + adam_eps)
    )
    master = weight.astype(jnp.float32)
    return (master - rate * (corrected + decay * master), first_new, second_new)


def reduce_group(grads):
    shares = (
        lax.psum_scatter(grads[0], "shard", scatter_dimension=0, tiled=True),
        lax.psum_scatter(grads[1], "shard", scatter_dimension=0, tiled=True),
        lax.psum_scatter(grads[2], "shard", scatter_dimension=0, tiled=True),
    )
    return lax.psum((shares[0], shares[1], shares[2]), "replica")


def on_device(
    tokens, cotangent, seq_lengths, w_in, w_out, w_small, m_in, v_in, m_out, v_out, m_small, v_small
):
    round_value, round_grad = make_rounders()
    full_in, full_out, full_small = (
        lax.all_gather(w_in, "shard", axis=0, tiled=True),
        lax.all_gather(w_out, "shard", axis=0, tiled=True),
        lax.all_gather(w_small, "shard", axis=0, tiled=True),
    )
    seglens = seq_lengths[0]

    def local(resid, weight_in, weight_out, packed):
        return mixer(resid, weight_in, weight_out, packed, seglens, round_value, round_grad)

    result, pullback = jax.vjp(
        local,
        tokens.astype(jnp.float32),
        full_in.astype(jnp.float32),
        full_out.astype(jnp.float32),
        full_small.astype(jnp.float32),
    )
    places = jnp.arange(tokens.shape[0], dtype=jnp.int32)
    valid = (places < tokens.shape[0] - seglens[-1]).astype(jnp.float32)[:, None]
    grad_x, grad_in, grad_out, grad_small = pullback(cotangent.astype(jnp.float32) * valid)
    share_in, share_out, share_small = reduce_group((grad_in, grad_out, grad_small))
    new_w_in, new_m_in, new_v_in = adamw(w_in, share_in, m_in, v_in, 0.05, 0.1)
    new_w_out, new_m_out, new_v_out = adamw(w_out, share_out, m_out, v_out, 0.04, 0.1)
    new_w_small, new_m_small, new_v_small = adamw(w_small, share_small, m_small, v_small, 0.3, 0.0)
    return (
        result.astype(jnp.bfloat16),
        grad_x.astype(jnp.bfloat16),
        new_w_in,
        new_m_in,
        new_v_in,
        new_w_out,
        new_m_out,
        new_v_out,
        new_w_small,
        new_m_small,
        new_v_small,
    )


CHAN = DI + 2 * STATE
HEADS = DI // HEAD
CIN = DI + CHAN + HEADS
MAIN = DI + CHAN
PADC = MAIN + 128
T = 128
PR = 48
OUT_W = 384
IN_W = 896
MESH = pl.DeviceIdType.MESH
VMEM_BYTES = 58 * 1024 * 1024
LAYER_BYTES = VMEM_BYTES
BF = jnp.bfloat16
F32 = jnp.float32


def place():
    replica, shard = lax.axis_index("replica"), lax.axis_index("shard")
    return replica // 2, replica % 2, shard // 2, shard % 2


def target(z, x, y, c):
    return (z * 2 + x, y * 2 + c)


def greet(peers):
    barrier = pltpu.get_barrier_semaphore()
    for peer in peers:
        pl.semaphore_signal(barrier, inc=1, device_id=peer, device_id_type=MESH)
    pl.semaphore_wait(barrier, len(peers))


def send(src, dst, send_sem, recv_sem, peer):
    copy = pltpu.make_async_remote_copy(
        src_ref=src, dst_ref=dst, send_sem=send_sem, recv_sem=recv_sem,
        device_id=peer, device_id_type=MESH,
    )
    copy.start()
    return copy


def gather_kernel(wi, sm, fi, fs, loc, s_own, r_own, s_y, r_y, s_x, r_x, s_sm, r_sm):
    z, x, y, c = place()
    core, other_y = target(z, x, y, 1 - c), target(z, x, 1 - y, c)
    diag, other_x = target(z, x, 1 - y, 1 - c), target(z, 1 - x, y, c)
    greet((core, other_y, diag, other_x))
    me = 2 * y + c
    far = (2 * (1 - y) + c, 2 * (1 - y) + 1 - c)
    small = [
        send(sm, fs.at[me], s_sm.at[i], r_sm.at[i], peer) for i, peer in enumerate((core, other_y, diag))
    ]
    over_y = []
    for u in range(GATHER):
        here = pl.ds(pl.multiple_of(x * 96 + 96 // GATHER * u, 16), 96 // GATHER)
        over_y.append([
            send(wi.at[here], fi.at[me, here], s_y.at[u, i], r_y.at[u, i], peer)
            for i, peer in enumerate((other_y, diag))
        ])
    own = send(wi, fi.at[me], s_own.at[0], r_own.at[0], core)
    keep = [
        pltpu.make_async_copy(src, full.at[me], loc.at[i])
        for i, (src, full) in enumerate(((wi, fi), (sm, fs)))
    ]
    for copy in keep:
        copy.start()
    over_x = []
    for u in range(GATHER):
        here = pl.ds(pl.multiple_of(x * 96 + 96 // GATHER * u, 16), 96 // GATHER)
        for i in range(2):
            over_y[u][i].wait_recv()
            part = fi.at[far[i], here]
            over_x.append(send(part, part, s_x.at[u, i], r_x.at[u, i], other_x))
    for copy in keep:
        copy.wait()
    for copy in small + [own] + over_x:
        copy.wait_recv()
    for copy in small + [own] + over_x + [copy for pair in over_y for copy in pair]:
        copy.wait_send()


GATHER = 3


def gather_weights(w_in, small):
    dma = pltpu.SemaphoreType.DMA
    return pl.pallas_call(
        gather_kernel,
        out_shape=(
            jax.ShapeDtypeStruct((4, 192, CIN), BF),
            jax.ShapeDtypeStruct((4, 32, 128), BF),
        ),
        in_specs=[pl.BlockSpec(memory_space=pl.ANY)] * 2,
        out_specs=[pl.BlockSpec(memory_space=pl.ANY)] * 2,
        scratch_shapes=[dma((2,)), dma((1,)), dma((1,)), dma((GATHER, 2)), dma((GATHER, 2)),
                        dma((GATHER, 2)), dma((GATHER, 2)), dma((3,)), dma((3,))],
        compiler_params=pltpu.CompilerParams(collective_id=0, has_side_effects=True),
        name="gather_weights",
    )(w_in, small)


def dot(a, b):
    return jnp.dot(a, b, preferred_element_type=F32)


def dot_nt(a, b):
    return lax.dot_general(a, b, (((1,), (1,)), ((), ())), preferred_element_type=F32)


def dot_tn(a, b):
    return lax.dot_general(a, b, (((0,), (0,)), ((), ())), preferred_element_type=F32)


def colsum(v):
    return jnp.sum(v, axis=0, keepdims=True)


def layer_kernel(
    x_ref, ct_ref, len_ref, wi_ref, wo_own, par_ref,
    out_ref, gx_ref, red_out, red_in, sm_out,
    gate, ci, conv, inner, scan, mixes, dproj, tail, nt, n2t, gated, n16, dact,
    dn2_all, dn2_out, out_part, out_in, d_own, d_in, n_in, n2_in, dp_in, own_out, half_out, quart_out, last_out,
    own_in, half_in, quart_in, last_in, gs, sbuf, srecv,
    s_o, r_o, s_w, r_w, s_d, r_d, s_n, r_n, s_2, r_2, s_p, r_p, s_r, r_r, s_s, r_s,
):
    z, x_at, y, c = place()
    core, other_y = target(z, x_at, y, 1 - c), target(z, x_at, 1 - y, c)
    diag, other_x = target(z, x_at, 1 - y, 1 - c), target(z, 1 - x_at, y, c)
    low, high = lax.rem(z, 2), z // 2
    near_z, far_z = target(2 * high + 1 - low, x_at, y, c), target(2 * (1 - high) + low, x_at, y, c)
    greet([core, other_y, diag, other_x, near_z, far_z])
    started = []

    def go(*args):
        copy = send(*args)
        started.append(copy)
        return copy

    me, far = 2 * y + c, 2 * (1 - y) + c
    group = [(core, 2 * y + 1 - c), (other_y, far), (diag, 2 * (1 - y) + 1 - c)]
    taps_ref, cb_ref = par_ref.at[0:4], par_ref.at[4:5]
    pg_ref, gg_ref = par_ref.at[5:6, 0:D], par_ref.at[6:7, 0:DI]
    step_bias, decay_log, skips = (par_ref[5:6, 768 + 128 * i:896 + 128 * i] for i in range(3))
    gs[...] = jnp.zeros(gs.shape, F32)
    bounds = [len_ref[0, 0]]
    for i in range(1, 4):
        bounds.append(bounds[-1] + len_ref[0, i])
    row = lax.broadcasted_iota(jnp.int32, (T, 1), 0)
    lane = lax.broadcasted_iota(jnp.int32, (1, T), 1)

    def segment(places):
        total = jnp.zeros(places.shape, jnp.int32)
        for bound in bounds:
            total = total + (places >= bound).astype(jnp.int32)
        return total

    seg_row, seg_lane = segment(row), segment(lane)
    within = [None] + [
        ((row >= j) & (segment(row - j) == seg_row)).astype(F32) for j in range(1, KCONV)
    ]
    allowed = (seg_row == seg_lane) & (row >= lane)
    valid = (row < bounds[2]).astype(F32)

    x = x_ref[...].astype(F32)
    r1 = lax.rsqrt(jnp.mean(x * x, axis=1, keepdims=True) + epsilon)
    normed = x * r1 * pg_ref[...]
    n16[...] = normed.astype(BF)
    nt[...] = normed.T.astype(BF).reshape(4, 192, T)
    dy = ct_ref[...].astype(F32) * valid
    d16 = dy.astype(BF)
    d_own[...] = d16
    d_got, n_got, n2_got = [], [], []
    for i, (peer, shard) in enumerate(group):
        d_got.append(go(d_own, d_in.at[i], s_d.at[i], r_d.at[i], peer))
    for i, (peer, shard) in enumerate(group):
        n_got.append(go(nt.at[shard], n_in.at[i], s_n.at[i], r_n.at[i], peer))
    dn2_all[me] = dot_nt(d16, wo_own[...]).astype(BF)
    tail[...] = jnp.zeros(tail.shape, BF)
    tail[:, :HEADS] = wi_ref[:, MAIN:]
    n = n16[...]
    step_in = dot(n, tail[...]) + step_bias
    for k in range(0, DI, 512):
        gate[:, k:k + 512] = dot(n, wi_ref[:, k:k + 512])
    W = 256
    for k in range(0, CHAN, W):
        cols = slice(k, k + W)
        v = dot(n, wi_ref[:, DI + k:DI + k + W])
        ci[:, cols] = v
        total = cb_ref[:, cols] + taps_ref[KCONV - 1:KCONV, cols] * v
        for j in range(1, KCONV):
            total = total + taps_ref[KCONV - 1 - j:KCONV - j, cols] * pltpu.roll(v, j, 0) * within[j]
        conv[:, cols] = total
        inner[:, cols] = (total * jax.nn.sigmoid(total)).astype(BF)
    dn2_got = []
    for i, (peer, shard) in enumerate(group):
        d_got[i].wait_recv()
        dn2_out[i] = dot_nt(d_in[i], wo_own[...]).astype(BF)
        dn2_got.append(go(dn2_out.at[i], dn2_all.at[me], s_w.at[i], r_w.at[i], peer))
    step = jnp.maximum(step_in, 0.0) + jnp.log1p(jnp.exp(-jnp.abs(step_in)))
    rate = -jnp.exp(decay_log)
    tri = (row >= lane).astype(F32)
    logs = jnp.dot(tri, step * rate, precision=lax.Precision.HIGHEST, preferred_element_type=F32)
    logs_t, step_t = logs.T, step.T
    in_state, out_state = inner[:, DI:DI + STATE], inner[:, DI + STATE:]
    inter = dot_nt(out_state, in_state)
    left = lane < HEAD

    def skip_of(q):
        return jnp.where(left, skips[:, 2 * q:2 * q + 1], skips[:, 2 * q + 1:2 * q + 2])

    gsq = jnp.zeros((T, 1), F32)
    for q in range(HEADS // 2):
        cols = slice(128 * q, 128 * q + 128)
        pair = inner[:, cols]
        parts = []
        for h in (2 * q, 2 * q + 1):
            spread = logs[:, h:h + 1] - logs_t[h:h + 1, :]
            decay = jnp.exp(jnp.where(allowed, spread, -1e30))
            mixes[h] = decay
            parts.append(dot((inter * decay * step_t[h:h + 1, :]).astype(BF), pair))
        value = jnp.where(left, parts[0], parts[1]) + pair.astype(F32) * skip_of(q)
        scan[:, cols] = value
        g = gate[:, cols]
        value = value * (g * jax.nn.sigmoid(g))
        gated[:, cols] = value
        gsq = gsq + jnp.sum(value * value, axis=1, keepdims=True)
    r2 = lax.rsqrt(gsq * (1.0 / DI) + epsilon)

    for k in range(0, DI, 128):
        n2t[k // 384, k % 384:k % 384 + 128, :] = (
            gated[:, k:k + 128] * r2 * gg_ref[:, k:k + 128]
        ).T.astype(BF)
    for i, (peer, shard) in enumerate(group):
        n2_got.append(go(n2t.at[shard], n2_in.at[i], s_2.at[i], r_2.at[i], peer))
    for copy in dn2_got:
        copy.wait_recv()
    mean_ug = jnp.zeros((T, 1), F32)
    W = 128
    for k in range(0, DI, W):
        cols = slice(k, k + W)
        g = gated[:, cols]
        dn2 = dn2_all[k // 384, :, k % 384:k % 384 + W].astype(F32)
        gs[6:7, cols] = colsum(dn2 * (g * r2))
        mean_ug = mean_ug + jnp.sum(dn2 * gg_ref[:, cols] * g, axis=1, keepdims=True)
    back = mean_ug * (1.0 / DI) * r2 * r2

    dinter = jnp.zeros((T, T), F32)
    dlog = jnp.zeros((T, T), F32)
    dskip = jnp.zeros((1, T), F32)
    dstep_rows, dlog_rows = [], []
    for q in range(HEADS // 2):
        cols = slice(128 * q, 128 * q + 128)
        g, value, gt = gate[:, cols], scan[:, cols], gated[:, cols]
        dgated = r2 * (dn2_all[q // 3, :, 128 * (q % 3):128 * (q % 3) + 128].astype(F32) * gg_ref[:, cols] - gt * back)
        sig = jax.nn.sigmoid(g)
        dscan = dgated * (g * sig)
        dproj[:, cols] = (dgated * value * (sig * (1.0 + g * (1.0 - sig)))).astype(BF)
        pair = inner[:, cols]
        pair32 = pair.astype(F32)
        by_lane = colsum(dscan * pair32)
        ds16 = dscan.astype(BF)
        parts = []
        for side, h in enumerate((2 * q, 2 * q + 1)):
            decay, srow = mixes[h], step_t[h:h + 1, :]
            mine = jnp.where(left if side == 0 else jnp.logical_not(left), pair32, 0.0).astype(BF)
            dmix = dot_nt(ds16, mine) * decay
            half = jnp.where(left if side == 0 else jnp.logical_not(left), by_lane, 0.0)
            dskip = dskip + jnp.where(lane == h, jnp.sum(half, axis=1, keepdims=True), 0.0)
            dinter = dinter + dmix * srow
            wide = dmix * inter
            per_source = colsum(wide)
            dstep_rows.append(per_source)
            dlog_rows.append(-per_source * srow)
            dlog = dlog + jnp.where(lane == h, jnp.sum(wide * srow, axis=1, keepdims=True), 0.0)
            parts.append(dot_tn((inter * decay * srow).astype(BF), ds16))
        dact[:, cols] = jnp.where(left, parts[0], parts[1]) + dscan * skip_of(q)
    def total_of(lefts, rights, cols):
        value = dot(lefts[0], rights[0][:, cols])
        for a, b in zip(lefts[1:], rights[1:]):
            value = value + dot(a, b[:, cols])
        return value

    class Piece:
        def __init__(self, own, red, p, half, quart, last):
            self.own, self.red, self.p = own, red, p
            self.half, self.quart, self.last = half.at[p], quart.at[p], last.at[p]
            self.sem = len(pieces_made)
            pieces_made.append(self)

        def go(self, step, src, dst, peer):
            self.copy = go(src, dst, s_r.at[step, self.sem], r_r.at[step, self.sem], peer)

        def add(self, dst, got):
            self.copy.wait_recv()
            for i in range(dst.shape[0]):
                at = dst.at[i]
                at[...] = (at[...].astype(F32) + got[i].astype(F32)).astype(BF)

        def over_x(self):
            self.go(0, self.own.at[1 - x_at, self.p], self.half, other_x)

        def near(self):
            mine = self.own.at[x_at, self.p]
            self.add(mine, self.half)
            self.go(1, mine.at[pl.ds(2 * (1 - low), 2)], self.quart, near_z)

        def far(self):
            mine = self.own.at[x_at, self.p]
            self.add(mine.at[pl.ds(2 * low, 2)], self.quart)
            self.go(2, mine.at[2 * low + 1 - high], self.last, far_z)

        def back_far(self):
            self.copy.wait_recv()
            at = 2 * low + high
            value = self.own[x_at, self.p, at].astype(F32) + self.last[...].astype(F32)
            self.red[x_at, self.p, at] = value.astype(BF)
            part = self.red.at[x_at, self.p, at]
            self.go(3, part, part, far_z)

        def back_near(self):
            self.copy.wait_recv()
            part = self.red.at[x_at, self.p, pl.ds(2 * low, 2)]
            self.go(4, part, part, near_z)

        def back_x(self):
            self.copy.wait_recv()
            part = self.red.at[x_at, self.p]
            self.go(5, part, part, other_x)

    pieces_made = []

    def spread_dproj(part, cols):
        return [
            go(dproj.at[:, cols], dp_in.at[i, :, cols], s_p.at[part, i], r_p.at[part, i], group[i][0])
            for i in range(2)
        ]

    dp_got = [spread_dproj(0, pl.ds(0, DI))]
    for copy in n2_got:
        copy.wait_recv()
    d_all = [d_own] + [d_in.at[i] for i in range(3)]
    n2_all = [n2t[me]] + [n2_in[i] for i in range(3)]
    for p in range(2):
        value = total_of(n2_all, d_all, slice(OUT_W * p, OUT_W * p + OUT_W)).astype(BF)
        own_out[:, p] = value.reshape(2, 4, PR, OUT_W)
    steps = [Piece(own_out, red_out, p, half_out, quart_out, last_out) for p in range(2)]
    for piece in steps:
        piece.over_x()
    rest = jnp.zeros((T - HEADS, T), F32)
    dstep = jnp.concatenate(dstep_rows + [rest], axis=0).T
    dlog = dlog + jnp.concatenate(dlog_rows + [rest], axis=0).T
    di16 = dinter.astype(BF)
    dact[:, DI:DI + STATE] = dot_tn(di16, out_state)
    dact[:, DI + STATE:] = dot(di16, in_state)
    upper = (row <= lane).astype(F32)
    ddecay = jnp.dot(upper, dlog, precision=lax.Precision.HIGHEST, preferred_element_type=F32)
    dstep = dstep + ddecay * rate
    draw = dstep * jax.nn.sigmoid(step_in)
    gs[5:6, 768:896] = colsum(draw)
    gs[5:6, 896:1024] = colsum(ddecay * step * rate)
    gs[5:6, 1024:1152] = dskip
    dproj[:, MAIN:] = draw.astype(BF)
    W = 256
    for k in range(0, CHAN, W):
        cols = slice(k, k + W)
        v, raw = conv[:, cols], ci[:, cols]
        sig = jax.nn.sigmoid(v)
        dconv = dact[:, cols] * (sig * (1.0 + v * (1.0 - sig)))
        gs[4:5, cols] = colsum(dconv)
        gs[KCONV - 1:KCONV, cols] = colsum(dconv * raw)
        dci = dconv * taps_ref[KCONV - 1:KCONV, cols]
        for j in range(1, KCONV):
            here = dconv * within[j]
            gs[KCONV - 1 - j:KCONV - j, cols] = colsum(here * pltpu.roll(raw, j, 0))
            dci = dci + pltpu.roll(here * taps_ref[KCONV - 1 - j:KCONV - j, cols], T - j, 0)
        dproj[:, DI + k:DI + k + W] = dci.astype(BF)

    dp_got.append(spread_dproj(1, pl.ds(DI, PADC - DI)))
    dn = dot_nt(dproj[:, MAIN:], tail[...])
    for k in range(0, MAIN, 256):
        dn = dn + dot_nt(dproj[:, k:k + 256], wi_ref[:, k:k + 256])
    xr = x * r1
    gs[5:6, 0:D] = colsum(dn * xr)
    u = dn * pg_ref[...]
    dx = r1 * (u - xr * jnp.mean(u * xr, axis=1, keepdims=True)) + dy
    gx_ref[...] = dx.astype(BF)

    small_copy = go(gs, srecv.at[0], s_s.at[0], r_s.at[0], core)
    for piece in steps:
        piece.near()
    forwarded = []
    for part, cols in enumerate((pl.ds(0, DI), pl.ds(DI, PADC - DI))):
        dp_got[part][1].wait_recv()
        forwarded.append(go(
            dp_in.at[1, :, cols], dp_in.at[2, :, cols], s_p.at[part, 2], r_p.at[part, 2], core
        ))
    for piece in steps:
        piece.far()
    for part in range(2):
        dp_got[part][0].wait_recv()
    for copy in n_got:
        copy.wait_recv()
    small_copy.wait_recv()
    sbuf[0] = gs[...] + srecv[0]
    small_copy = go(sbuf.at[0], srecv.at[1], s_s.at[1], r_s.at[1], other_y)
    for piece in steps:
        piece.back_far()
    n_all = [nt[me]] + [n_in[i] for i in range(3)]
    dp_all = [dproj] + [dp_in.at[i] for i in range(3)]

    def put(k, first, value):
        wide = value.shape[1]
        own_in[:, :, k, :, first:first + wide] = value.astype(BF).reshape(2, 2, PR, wide)

    forwarded[0].wait_recv()
    put(0, 0, total_of(n_all, dp_all, slice(0, IN_W)))
    forwarded[1].wait_recv()
    for k in range(1, 3):
        put(k, 0, total_of(n_all, dp_all, slice(IN_W * k, IN_W * k + IN_W)))
    put(3, 0, total_of(n_all, dp_all, slice(IN_W * 3, PADC)))
    put(3, PADC - 3 * IN_W, jnp.zeros((192, 4 * IN_W - PADC), F32))
    main = [Piece(own_in, red_in, p, half_in, quart_in, last_in) for p in range(2)]
    for piece in main:
        piece.over_x()
    for piece in steps:
        piece.back_near()
    out_got = []
    for i, (peer, shard) in enumerate(group):
        out_part[i] = dot_tn(n2_in[i], wo_own[...]).astype(BF)
        out_got.append(go(out_part.at[i], out_in.at[i], s_o.at[i], r_o.at[i], peer))
    for s, (peer, piece_step) in enumerate(((other_x, "near"), (near_z, "far"), (far_z, "back_far"))):
        for piece in main:
            getattr(piece, piece_step)()
        small_copy.wait_recv()
        sbuf[s + 1] = sbuf[s] + srecv[s + 1]
        small_copy = go(sbuf.at[s + 1], srecv.at[s + 2], s_s.at[s + 2], r_s.at[s + 2], peer)
    for piece in steps:
        piece.back_x()
    for piece in main:
        piece.back_near()
    out = x_ref[...].astype(F32) + dot_tn(n2t[me], wo_own[...])
    for i in range(3):
        out_got[i].wait_recv()
        out = out + out_in[i].astype(F32)
    out_ref[...] = out.astype(BF)
    for piece in main:
        piece.back_x()
    small_copy.wait_recv()
    sm_out[...] = sbuf[3] + srecv[4]
    for piece in steps + main:
        piece.copy.wait_recv()
    for copy in started:
        copy.wait_send()


def layer(tokens, cotangent, lens, w_in, w_out, params):
    vmem = pl.BlockSpec(memory_space=pltpu.VMEM)
    shape = jax.ShapeDtypeStruct
    dma = pltpu.SemaphoreType.DMA
    return pl.pallas_call(
        layer_kernel,
        out_shape=(
            shape((T, D), BF), shape((T, D), BF), shape((2, 2, 4, PR, OUT_W), BF),
            shape((2, 2, 4, PR, IN_W), BF), shape((8, CHAN), F32),
        ),
        in_specs=[vmem, vmem, pl.BlockSpec(memory_space=pltpu.SMEM)] + [vmem] * 3,
        out_specs=[vmem] * 5,
        scratch_shapes=[
            pltpu.VMEM((T, DI), F32), pltpu.VMEM((T, CHAN), F32), pltpu.VMEM((T, CHAN), F32),
            pltpu.VMEM((T, CHAN), BF), pltpu.VMEM((T, DI), F32), pltpu.VMEM((HEADS, T, T), F32),
            pltpu.VMEM((T, PADC), BF), pltpu.VMEM((D, 128), BF), pltpu.VMEM((4, 192, T), BF),
            pltpu.VMEM((4, 384, T), BF), pltpu.VMEM((T, DI), F32), pltpu.VMEM((T, D), BF),
            pltpu.VMEM((T, CHAN), F32),
            pltpu.VMEM((4, T, 384), BF), pltpu.VMEM((3, T, 384), BF), pltpu.VMEM((3, T, D), BF),
            pltpu.VMEM((3, T, D), BF), pltpu.VMEM((T, D), BF), pltpu.VMEM((3, T, D), BF),
            pltpu.VMEM((3, 192, T), BF), pltpu.VMEM((3, 384, T), BF), pltpu.VMEM((3, T, PADC), BF),
            pltpu.VMEM((2, 2, 4, PR, OUT_W), BF), pltpu.VMEM((2, 4, PR, OUT_W), BF),
            pltpu.VMEM((2, 2, PR, OUT_W), BF), pltpu.VMEM((2, PR, OUT_W), BF),
            pltpu.VMEM((2, 2, 4, PR, IN_W), BF), pltpu.VMEM((2, 4, PR, IN_W), BF),
            pltpu.VMEM((2, 2, PR, IN_W), BF), pltpu.VMEM((2, PR, IN_W), BF),
            pltpu.VMEM((8, CHAN), F32), pltpu.VMEM((4, 8, CHAN), F32), pltpu.VMEM((5, 8, CHAN), F32),
            dma((3,)), dma((3,)), dma((3,)), dma((3,)), dma((3,)), dma((3,)), dma((3,)), dma((3,)), dma((3,)), dma((3,)),
            dma((2, 3)), dma((2, 3)), dma((6, 4)), dma((6, 4)), dma((5,)), dma((5,)),
        ],
        compiler_params=pltpu.CompilerParams(
            collective_id=1, has_side_effects=True, vmem_limit_bytes=LAYER_BYTES
        ),
        name="layer",
    )(tokens, cotangent, lens, w_in, w_out, params)


def adamw_kernel(red_out, red_in, wi, mi, vi, wo, mo, vo, nwi, nmi, nvi, nwo, nmo, nvo):
    def update(cols, grad, refs, rate, part):
        at = (part, cols)
        gradient, master = grad.astype(F32), refs[0][at].astype(F32)
        first = beta_one * refs[1][at] + (1.0 - beta_one) * gradient
        second = beta_two * refs[2][at] + (1.0 - beta_two) * gradient * gradient
        root = jnp.sqrt(second * (1.0 / (1.0 - beta_two**STEP))) + adam_eps
        scale = rate / (1.0 - beta_one**STEP)
        new = (master * (1.0 - rate * 0.1) - scale * first / root, first, second)
        for ref, value in zip(refs[3:], new):
            ref[at] = value

    refs_in = (wi, mi, vi, nwi, nmi, nvi)
    refs_out = (wo, mo, vo, nwo, nmo, nvo)
    for k in range(4):
        wide = min(IN_W, CIN - IN_W * k)
        update(slice(IN_W * k, IN_W * k + wide), red_in[0, 0, k, :, :wide], refs_in, 0.05, slice(None))
    for p in range(2):
        for k in range(2):
            update(
                slice(OUT_W * p, OUT_W * p + OUT_W), red_out[0, p, k], refs_out, 0.04,
                slice(PR * k, PR * k + PR),
            )


def adamw_all(red_out, red_in, w_in, m_in, v_in, w_out, m_out, v_out):
    spec_in = pl.BlockSpec((PR, CIN), lambda i: (i, 0))
    spec_out = pl.BlockSpec((2 * PR, D), lambda i: (i, 0))
    return pl.pallas_call(
        adamw_kernel,
        grid=(4,),
        out_shape=[jax.ShapeDtypeStruct((192, CIN), F32)] * 3 + [jax.ShapeDtypeStruct((384, D), F32)] * 3,
        in_specs=[
            pl.BlockSpec((1, 2, 2, PR, OUT_W), lambda i: (i // 2, 0, i % 2, 0, 0)),
            pl.BlockSpec((1, 1, 4, PR, IN_W), lambda i: (i // 2, i % 2, 0, 0, 0)),
        ] + [spec_in] * 3 + [spec_out] * 3,
        out_specs=[spec_in] * 3 + [spec_out] * 3,
        compiler_params=pltpu.CompilerParams(vmem_limit_bytes=VMEM_BYTES),
        name="adamw",
    )(red_out, red_in, w_in, m_in, v_in, w_out, m_out, v_out)


def on_device_fast(
    tokens, cotangent, seq_lengths, w_in, w_out, w_small, m_in, v_in, m_out, v_out, m_small, v_small
):
    share = w_small.shape[0]
    small = jnp.pad(w_small, (0, 32 * 128 - share)).reshape(32, 128)
    full_in, full_small = gather_weights(w_in, small)
    packed = full_small.reshape(4, 32 * 128)[:, :share].reshape(4 * share).astype(F32)
    start = (KCONV + 1) * CHAN
    gains = start + 3 * HEADS
    heads = jnp.pad(packed[start:gains].reshape(3, HEADS), ((0, 0), (0, 128 - HEADS)))
    params = jnp.concatenate([
        packed[:start], packed[gains : gains + D], heads.reshape(-1), jnp.zeros(CHAN - D - 384, F32),
        packed[gains + D :], jnp.zeros(2 * CHAN - DI, F32),
    ]).reshape(8, CHAN)
    out, gx, red_out, red_in, sums = layer(
        tokens, cotangent, seq_lengths, full_in.reshape(D, CIN), w_out, params
    )
    flat = jnp.concatenate([
        sums[:5].reshape(-1), sums[5, D : D + HEADS], sums[5, D + 128 : D + 128 + HEADS],
        sums[5, D + 256 : D + 256 + HEADS], sums[5, :D], sums[6, :DI],
    ])
    share_small = lax.dynamic_slice_in_dim(flat, lax.axis_index("shard") * share, share)
    new = adamw_all(red_out, red_in, w_in, m_in, v_in, w_out, m_out, v_out)
    new_small = adamw(w_small, share_small, m_small, v_small, 0.3, 0.0)
    return (out, gx, *new, *new_small)


def solution(mesh):
    in_specs = (
        P(("replica", "shard"), None),
        P(("replica", "shard"), None),
        P(("replica", "shard"), None),
        P("shard", None),
        P("shard", None),
        P("shard"),
        P("shard", None),
        P("shard", None),
        P("shard", None),
        P("shard", None),
        P("shard"),
        P("shard"),
    )
    out_specs = (
        P(("replica", "shard"), None),
        P(("replica", "shard"), None),
        P("shard", None),
        P("shard", None),
        P("shard", None),
        P("shard", None),
        P("shard", None),
        P("shard", None),
        P("shard"),
        P("shard"),
        P("shard"),
    )
    fast = dict(mesh.shape) == {"replica": 8, "shard": 4}
    return jax.shard_map(
        on_device_fast if fast else on_device, mesh=mesh, in_specs=in_specs, out_specs=out_specs, check_vma=False
    )
```

```python
import jax
import jax.numpy as jnp
from jax import lax
from jax.experimental import pallas as pl
from jax.experimental.pallas import tpu as pltpu
from jax.sharding import PartitionSpec as P

D = 768
STATE = 128
HEAD = 64
KCONV = 4
STEP = 10
DI = 1536


epsilon = 1e-05
beta_one = 0.9
beta_two = 0.95
adam_eps = 1e-08


def make_rounders():

    def round_plain(value):
        return lax.optimization_barrier(value.astype(jnp.bfloat16)).astype(jnp.float32)

    def unchanged(value):
        return value

    round_value = jax.custom_vjp(round_plain)
    round_grad = jax.custom_vjp(unchanged)

    def value_keep(value):
        return (round_plain(value), None)

    def value_pass(kept, gradient):
        return (gradient,)

    def grad_keep(value):
        return (value, None)

    def grad_round(kept, gradient):
        return (round_plain(gradient),)

    round_value.defvjp(value_keep, value_pass)
    round_grad.defvjp(grad_keep, grad_round)
    return (round_value, round_grad)


def mixer(resid, weight_in, weight_out, packed, seglens, round_value, round_grad):
    rows_count = resid.shape[0]
    channels = DI + 2 * STATE
    heads = DI // HEAD
    kernel = packed[: KCONV * channels].reshape(KCONV, channels)
    conv_bias = packed[KCONV * channels : (KCONV + 1) * channels]
    start = (KCONV + 1) * channels
    step_bias = packed[start : start + heads]
    decay_log = packed[start + heads : start + 2 * heads]
    skip_gain = packed[start + 2 * heads : start + 3 * heads]
    pre_gain = packed[start + 3 * heads : start + 3 * heads + D]
    gate_gain = packed[start + 3 * heads + D :]
    places = jnp.arange(rows_count, dtype=jnp.int32)
    bounds = jnp.cumsum(seglens)
    segment = jnp.sum((places[:, None] >= bounds[None, :]).astype(jnp.int32), axis=1)
    meansq = jnp.mean(resid * resid, axis=1, keepdims=True)
    normed = resid * lax.rsqrt(meansq + epsilon) * pre_gain
    project = round_grad(
        jnp.dot(round_value(normed), weight_in, preferred_element_type=jnp.float32)
    )
    gate_raw = project[:, :DI]
    conv_in = project[:, DI : DI + channels]
    step_raw = project[:, DI + channels :]
    convolved = conv_bias + kernel[KCONV - 1] * conv_in
    for offset in range(1, KCONV):
        shifted = jnp.concatenate(
            [jnp.zeros((offset, channels), jnp.float32), conv_in[:-offset]], axis=0
        )
        earlier = jnp.concatenate([jnp.full((offset,), -1, jnp.int32), segment[:-offset]])
        within = (earlier == segment).astype(jnp.float32)[:, None]
        convolved = convolved + kernel[KCONV - 1 - offset] * shifted * within
    activated = jax.nn.silu(convolved)
    inner = round_value(activated[:, :DI])
    in_state = round_value(activated[:, DI : DI + STATE])
    out_state = round_value(activated[:, DI + STATE :])
    step_size = jax.nn.softplus(step_raw + step_bias)
    logrates = jnp.cumsum(step_size * -jnp.exp(decay_log), axis=0)
    intersection = round_grad(jnp.dot(out_state, in_state.T, preferred_element_type=jnp.float32))
    allowed = (segment[:, None] == segment[None, :]) & (places[:, None] >= places[None, :])
    group_count = heads // 8
    rates_grouped = logrates.reshape(rows_count, group_count, 8).transpose(1, 0, 2)
    steps_grouped = step_size.reshape(rows_count, group_count, 8).transpose(1, 0, 2)
    inner_grouped = inner.reshape(rows_count, group_count, 8, HEAD).transpose(1, 0, 2, 3)

    def mix_group(entry):
        rate_part, step_part, inner_part = entry
        spread = rate_part.T[:, :, None] - rate_part.T[:, None, :]
        weights = round_value(
            intersection[None]
            * jnp.exp(jnp.where(allowed[None], spread, -1e30))
            * step_part.T[:, None, :]
        )
        return jnp.einsum("hts,shp->thp", weights, inner_part, preferred_element_type=jnp.float32)

    mixed = lax.map(jax.checkpoint(mix_group), (rates_grouped, steps_grouped, inner_grouped))
    scanned = round_grad(mixed.transpose(1, 0, 2, 3).reshape(rows_count, DI)) + inner * jnp.repeat(
        skip_gain, HEAD
    )
    gated = scanned * jax.nn.silu(gate_raw)
    gatesq = jnp.mean(gated * gated, axis=1, keepdims=True)
    normed_two = gated * lax.rsqrt(gatesq + epsilon) * gate_gain
    output = round_grad(
        jnp.dot(round_value(normed_two), weight_out, preferred_element_type=jnp.float32)
    )
    return resid + output


def adamw(weight, gradient, first, second, rate, decay):
    first_new = beta_one * first + (1.0 - beta_one) * gradient
    second_new = beta_two * second + (1.0 - beta_two) * gradient * gradient
    corrected = (
        first_new
        / (1.0 - beta_one**STEP)
        / (jnp.sqrt(second_new / (1.0 - beta_two**STEP)) + adam_eps)
    )
    master = weight.astype(jnp.float32)
    return (master - rate * (corrected + decay * master), first_new, second_new)


def reduce_group(grads):
    shares = (
        lax.psum_scatter(grads[0], "shard", scatter_dimension=0, tiled=True),
        lax.psum_scatter(grads[1], "shard", scatter_dimension=0, tiled=True),
        lax.psum_scatter(grads[2], "shard", scatter_dimension=0, tiled=True),
    )
    return lax.psum((shares[0], shares[1], shares[2]), "replica")


def on_device(
    tokens, cotangent, seq_lengths, w_in, w_out, w_small, m_in, v_in, m_out, v_out, m_small, v_small
):
    round_value, round_grad = make_rounders()
    full_in, full_out, full_small = (
        lax.all_gather(w_in, "shard", axis=0, tiled=True),
        lax.all_gather(w_out, "shard", axis=0, tiled=True),
        lax.all_gather(w_small, "shard", axis=0, tiled=True),
    )
    seglens = seq_lengths[0]

    def local(resid, weight_in, weight_out, packed):
        return mixer(resid, weight_in, weight_out, packed, seglens, round_value, round_grad)

    result, pullback = jax.vjp(
        local,
        tokens.astype(jnp.float32),
        full_in.astype(jnp.float32),
        full_out.astype(jnp.float32),
        full_small.astype(jnp.float32),
    )
    places = jnp.arange(tokens.shape[0], dtype=jnp.int32)
    valid = (places < tokens.shape[0] - seglens[-1]).astype(jnp.float32)[:, None]
    grad_x, grad_in, grad_out, grad_small = pullback(cotangent.astype(jnp.float32) * valid)
    share_in, share_out, share_small = reduce_group((grad_in, grad_out, grad_small))
    new_w_in, new_m_in, new_v_in = adamw(w_in, share_in, m_in, v_in, 0.05, 0.1)
    new_w_out, new_m_out, new_v_out = adamw(w_out, share_out, m_out, v_out, 0.04, 0.1)
    new_w_small, new_m_small, new_v_small = adamw(w_small, share_small, m_small, v_small, 0.3, 0.0)
    return (
        result.astype(jnp.bfloat16),
        grad_x.astype(jnp.bfloat16),
        new_w_in,
        new_m_in,
        new_v_in,
        new_w_out,
        new_m_out,
        new_v_out,
        new_w_small,
        new_m_small,
        new_v_small,
    )


CHAN = DI + 2 * STATE
HEADS = DI // HEAD
CIN = DI + CHAN + HEADS
MAIN = DI + CHAN
PADC = MAIN + 128
T = 128
PR = 48
OUT_W = 384
IN_W = 896
MESH = pl.DeviceIdType.MESH
VMEM_BYTES = 58 * 1024 * 1024
LAYER_BYTES = VMEM_BYTES
BF = jnp.bfloat16
F32 = jnp.float32


def place():
    replica, shard = lax.axis_index("replica"), lax.axis_index("shard")
    return replica // 2, replica % 2, shard // 2, shard % 2


def target(z, x, y, c):
    return (z * 2 + x, y * 2 + c)


def greet(peers):
    barrier = pltpu.get_barrier_semaphore()
    for peer in peers:
        pl.semaphore_signal(barrier, inc=1, device_id=peer, device_id_type=MESH)
    pl.semaphore_wait(barrier, len(peers))


def send(src, dst, send_sem, recv_sem, peer):
    copy = pltpu.make_async_remote_copy(
        src_ref=src, dst_ref=dst, send_sem=send_sem, recv_sem=recv_sem,
        device_id=peer, device_id_type=MESH,
    )
    copy.start()
    return copy


def gather_kernel(wi, sm, fi, fs, loc, s_own, r_own, s_y, r_y, s_x, r_x, s_sm, r_sm):
    z, x, y, c = place()
    core, other_y = target(z, x, y, 1 - c), target(z, x, 1 - y, c)
    diag, other_x = target(z, x, 1 - y, 1 - c), target(z, 1 - x, y, c)
    greet((core, other_y, diag, other_x))
    me = 2 * y + c
    far = (2 * (1 - y) + c, 2 * (1 - y) + 1 - c)
    small = [
        send(sm, fs.at[me], s_sm.at[i], r_sm.at[i], peer) for i, peer in enumerate((core, other_y, diag))
    ]
    over_y = []
    for u in range(GATHER):
        here = pl.ds(pl.multiple_of(x * 96 + 96 // GATHER * u, 16), 96 // GATHER)
        over_y.append([
            send(wi.at[here], fi.at[me, here], s_y.at[u, i], r_y.at[u, i], peer)
            for i, peer in enumerate((other_y, diag))
        ])
    own = send(wi, fi.at[me], s_own.at[0], r_own.at[0], core)
    keep = [
        pltpu.make_async_copy(src, full.at[me], loc.at[i])
        for i, (src, full) in enumerate(((wi, fi), (sm, fs)))
    ]
    for copy in keep:
        copy.start()
    over_x = []
    for u in range(GATHER):
        here = pl.ds(pl.multiple_of(x * 96 + 96 // GATHER * u, 16), 96 // GATHER)
        for i in range(2):
            over_y[u][i].wait_recv()
            part = fi.at[far[i], here]
            over_x.append(send(part, part, s_x.at[u, i], r_x.at[u, i], other_x))
    for copy in keep:
        copy.wait()
    for copy in small + [own] + over_x:
        copy.wait_recv()
    for copy in small + [own] + over_x + [copy for pair in over_y for copy in pair]:
        copy.wait_send()


GATHER = 3


def gather_weights(w_in, small):
    dma = pltpu.SemaphoreType.DMA
    return pl.pallas_call(
        gather_kernel,
        out_shape=(
            jax.ShapeDtypeStruct((4, 192, CIN), BF),
            jax.ShapeDtypeStruct((4, 32, 128), BF),
        ),
        in_specs=[pl.BlockSpec(memory_space=pl.ANY)] * 2,
        out_specs=[pl.BlockSpec(memory_space=pl.ANY)] * 2,
        scratch_shapes=[dma((2,)), dma((1,)), dma((1,)), dma((GATHER, 2)), dma((GATHER, 2)),
                        dma((GATHER, 2)), dma((GATHER, 2)), dma((3,)), dma((3,))],
        compiler_params=pltpu.CompilerParams(collective_id=0, has_side_effects=True),
        name="gather_weights",
    )(w_in, small)


def dot(a, b):
    return jnp.dot(a, b, preferred_element_type=F32)


def dot_nt(a, b):
    return lax.dot_general(a, b, (((1,), (1,)), ((), ())), preferred_element_type=F32)


def dot_tn(a, b):
    return lax.dot_general(a, b, (((0,), (0,)), ((), ())), preferred_element_type=F32)


def colsum(v):
    return jnp.sum(v, axis=0, keepdims=True)


def layer_kernel(
    x_ref, ct_ref, len_ref, wi_ref, wo_own, par_ref,
    out_ref, gx_ref, red_out, red_in, sm_out,
    gate, ci, conv, inner, scan, mixes, dproj, tail, nt, n2t, gated, n16, dact,
    dn2_all, dn2_out, out_part, out_in, d_own, d_in, n_in, n2_in, dp_in, own_out, half_out, quart_out, last_out,
    own_in, half_in, quart_in, last_in, gs, sbuf, srecv,
    s_o, r_o, s_w, r_w, s_d, r_d, s_n, r_n, s_2, r_2, s_p, r_p, s_r, r_r, s_s, r_s,
):
    z, x_at, y, c = place()
    core, other_y = target(z, x_at, y, 1 - c), target(z, x_at, 1 - y, c)
    diag, other_x = target(z, x_at, 1 - y, 1 - c), target(z, 1 - x_at, y, c)
    low, high = lax.rem(z, 2), z // 2
    near_z, far_z = target(2 * high + 1 - low, x_at, y, c), target(2 * (1 - high) + low, x_at, y, c)
    greet([core, other_y, diag, other_x, near_z, far_z])
    started = []

    def go(*args):
        copy = send(*args)
        started.append(copy)
        return copy

    me, far = 2 * y + c, 2 * (1 - y) + c
    group = [(core, 2 * y + 1 - c), (other_y, far), (diag, 2 * (1 - y) + 1 - c)]
    taps_ref, cb_ref = par_ref.at[0:4], par_ref.at[4:5]
    pg_ref, gg_ref = par_ref.at[5:6, 0:D], par_ref.at[6:7, 0:DI]
    step_bias, decay_log, skips = (par_ref[5:6, 768 + 128 * i:896 + 128 * i] for i in range(3))
    gs[...] = jnp.zeros(gs.shape, F32)
    bounds = [len_ref[0, 0]]
    for i in range(1, 4):
        bounds.append(bounds[-1] + len_ref[0, i])
    row = lax.broadcasted_iota(jnp.int32, (T, 1), 0)
    lane = lax.broadcasted_iota(jnp.int32, (1, T), 1)

    def segment(places):
        total = jnp.zeros(places.shape, jnp.int32)
        for bound in bounds:
            total = total + (places >= bound).astype(jnp.int32)
        return total

    seg_row, seg_lane = segment(row), segment(lane)
    within = [None] + [
        ((row >= j) & (segment(row - j) == seg_row)).astype(F32) for j in range(1, KCONV)
    ]
    allowed = (seg_row == seg_lane) & (row >= lane)
    valid = (row < bounds[2]).astype(F32)

    x = x_ref[...].astype(F32)
    r1 = lax.rsqrt(jnp.mean(x * x, axis=1, keepdims=True) + epsilon)
    normed = x * r1 * pg_ref[...]
    n16[...] = normed.astype(BF)
    nt[...] = normed.T.astype(BF).reshape(4, 192, T)
    dy = ct_ref[...].astype(F32) * valid
    d16 = dy.astype(BF)
    d_own[...] = d16
    d_got, n_got, n2_got = [], [], []
    for i, (peer, shard) in enumerate(group):
        d_got.append(go(d_own, d_in.at[i], s_d.at[i], r_d.at[i], peer))
    for i, (peer, shard) in enumerate(group):
        n_got.append(go(nt.at[shard], n_in.at[i], s_n.at[i], r_n.at[i], peer))
    dn2_all[me] = dot_nt(d16, wo_own[...]).astype(BF)
    tail[...] = jnp.zeros(tail.shape, BF)
    tail[:, :HEADS] = wi_ref[:, MAIN:]
    n = n16[...]
    step_in = dot(n, tail[...]) + step_bias
    for k in range(0, DI, 512):
        gate[:, k:k + 512] = dot(n, wi_ref[:, k:k + 512])
    W = 256
    for k in range(0, CHAN, W):
        cols = slice(k, k + W)
        v = dot(n, wi_ref[:, DI + k:DI + k + W])
        ci[:, cols] = v
        total = cb_ref[:, cols] + taps_ref[KCONV - 1:KCONV, cols] * v
        for j in range(1, KCONV):
            total = total + taps_ref[KCONV - 1 - j:KCONV - j, cols] * pltpu.roll(v, j, 0) * within[j]
        conv[:, cols] = total
        inner[:, cols] = (total * jax.nn.sigmoid(total)).astype(BF)
    dn2_got = []
    for i, (peer, shard) in enumerate(group):
        d_got[i].wait_recv()
        dn2_out[i] = dot_nt(d_in[i], wo_own[...]).astype(BF)
        dn2_got.append(go(dn2_out.at[i], dn2_all.at[me], s_w.at[i], r_w.at[i], peer))
    step = jnp.maximum(step_in, 0.0) + jnp.log1p(jnp.exp(-jnp.abs(step_in)))
    rate = -jnp.exp(decay_log)
    tri = (row >= lane).astype(F32)
    logs = jnp.dot(tri, step * rate, precision=lax.Precision.HIGHEST, preferred_element_type=F32)
    logs_t, step_t = logs.T, step.T
    in_state, out_state = inner[:, DI:DI + STATE], inner[:, DI + STATE:]
    inter = dot_nt(out_state, in_state)
    left = lane < HEAD

    def skip_of(q):
        return jnp.where(left, skips[:, 2 * q:2 * q + 1], skips[:, 2 * q + 1:2 * q + 2])

    gsq = jnp.zeros((T, 1), F32)
    for q in range(HEADS // 2):
        cols = slice(128 * q, 128 * q + 128)
        pair = inner[:, cols]
        parts = []
        for h in (2 * q, 2 * q + 1):
            spread = logs[:, h:h + 1] - logs_t[h:h + 1, :]
            decay = jnp.exp(jnp.where(allowed, spread, -1e30))
            mixes[h] = decay
            parts.append(dot((inter * decay * step_t[h:h + 1, :]).astype(BF), pair))
        value = jnp.where(left, parts[0], parts[1]) + pair.astype(F32) * skip_of(q)
        scan[:, cols] = value
        g = gate[:, cols]
        value = value * (g * jax.nn.sigmoid(g))
        gated[:, cols] = value
        gsq = gsq + jnp.sum(value * value, axis=1, keepdims=True)
    r2 = lax.rsqrt(gsq * (1.0 / DI) + epsilon)

    for k in range(0, DI, 128):
        n2t[k // 384, k % 384:k % 384 + 128, :] = (
            gated[:, k:k + 128] * r2 * gg_ref[:, k:k + 128]
        ).T.astype(BF)
    for i, (peer, shard) in enumerate(group):
        n2_got.append(go(n2t.at[shard], n2_in.at[i], s_2.at[i], r_2.at[i], peer))
    for copy in dn2_got:
        copy.wait_recv()
    mean_ug = jnp.zeros((T, 1), F32)
    W = 128
    for k in range(0, DI, W):
        cols = slice(k, k + W)
        g = gated[:, cols]
        dn2 = dn2_all[k // 384, :, k % 384:k % 384 + W].astype(F32)
        gs[6:7, cols] = colsum(dn2 * (g * r2))
        mean_ug = mean_ug + jnp.sum(dn2 * gg_ref[:, cols] * g, axis=1, keepdims=True)
    back = mean_ug * (1.0 / DI) * r2 * r2

    dinter = jnp.zeros((T, T), F32)
    dlog = jnp.zeros((T, T), F32)
    dskip = jnp.zeros((1, T), F32)
    dstep_rows, dlog_rows = [], []
    for q in range(HEADS // 2):
        cols = slice(128 * q, 128 * q + 128)
        g, value, gt = gate[:, cols], scan[:, cols], gated[:, cols]
        dgated = r2 * (dn2_all[q // 3, :, 128 * (q % 3):128 * (q % 3) + 128].astype(F32) * gg_ref[:, cols] - gt * back)
        sig = jax.nn.sigmoid(g)
        dscan = dgated * (g * sig)
        dproj[:, cols] = (dgated * value * (sig * (1.0 + g * (1.0 - sig)))).astype(BF)
        pair = inner[:, cols]
        pair32 = pair.astype(F32)
        by_lane = colsum(dscan * pair32)
        ds16 = dscan.astype(BF)
        parts = []
        for side, h in enumerate((2 * q, 2 * q + 1)):
            decay, srow = mixes[h], step_t[h:h + 1, :]
            mine = jnp.where(left if side == 0 else jnp.logical_not(left), pair32, 0.0).astype(BF)
            dmix = dot_nt(ds16, mine) * decay
            half = jnp.where(left if side == 0 else jnp.logical_not(left), by_lane, 0.0)
            dskip = dskip + jnp.where(lane == h, jnp.sum(half, axis=1, keepdims=True), 0.0)
            dinter = dinter + dmix * srow
            wide = dmix * inter
            per_source = colsum(wide)
            dstep_rows.append(per_source)
            dlog_rows.append(-per_source * srow)
            dlog = dlog + jnp.where(lane == h, jnp.sum(wide * srow, axis=1, keepdims=True), 0.0)
            parts.append(dot_tn((inter * decay * srow).astype(BF), ds16))
        dact[:, cols] = jnp.where(left, parts[0], parts[1]) + dscan * skip_of(q)
    def total_of(lefts, rights, cols):
        value = dot(lefts[0], rights[0][:, cols])
        for a, b in zip(lefts[1:], rights[1:]):
            value = value + dot(a, b[:, cols])
        return value

    class Piece:
        def __init__(self, own, red, p, half, quart, last):
            self.own, self.red, self.p = own, red, p
            self.half, self.quart, self.last = half.at[p], quart.at[p], last.at[p]
            self.sem = len(pieces_made)
            pieces_made.append(self)

        def go(self, step, peer, *pairs):
            self.copies = [
                go(src, dst, s_r.at[step, self.sem, i], r_r.at[step, self.sem, i], peer)
                for i, (src, dst) in enumerate(pairs)
            ]

        def arrive(self):
            for copy in self.copies:
                copy.wait_recv()

        def add(self, dst, got):
            for i in range(dst.shape[0]):
                at = dst.at[i]
                at[...] = (at[...].astype(F32) + got[i].astype(F32)).astype(BF)

        def finish(self, peer):
            at = 2 * low + high
            value = self.own[x_at, self.p, at].astype(F32) + self.last[...].astype(F32)
            self.red[x_at, self.p, at] = value.astype(BF)
            part = self.red.at[x_at, self.p, at]
            self.go(3, peer, (part, part))

        def share(self, step, peer, *parts):
            self.arrive()
            self.go(step, peer, *[(part, part) for part in parts])

    class XFirst(Piece):
        def over_x(self):
            self.go(0, other_x, (self.own.at[1 - x_at, self.p], self.half))

        def near(self):
            mine = self.own.at[x_at, self.p]
            self.arrive()
            self.add(mine, self.half)
            self.go(1, near_z, (mine.at[pl.ds(2 * (1 - low), 2)], self.quart))

        def far(self):
            mine = self.own.at[x_at, self.p]
            self.arrive()
            self.add(mine.at[pl.ds(2 * low, 2)], self.quart)
            self.go(2, far_z, (mine.at[2 * low + 1 - high], self.last))

        def back_far(self):
            self.arrive()
            self.finish(far_z)

        def back_near(self):
            self.share(4, near_z, self.red.at[x_at, self.p, pl.ds(2 * low, 2)])

        def back_x(self):
            self.share(5, other_x, self.red.at[x_at, self.p])

    class ZFirst(Piece):
        def over_x(self):
            away = pl.ds(2 * (1 - low), 2)
            self.go(0, near_z, *[
                (self.own.at[i, self.p, away], self.half.at[pl.ds(2 * i, 2)]) for i in range(2)
            ])

        def near(self):
            self.arrive()
            for i in range(2):
                self.add(self.own.at[i, self.p, pl.ds(2 * low, 2)], self.half.at[pl.ds(2 * i, 2)])
            away = 2 * low + 1 - high
            self.go(1, far_z, *[(self.own.at[i, self.p, away], self.quart.at[i]) for i in range(2)])

        def far(self):
            self.arrive()
            at = 2 * low + high
            for i in range(2):
                self.add(self.own.at[i, self.p, pl.ds(at, 1)], self.quart.at[pl.ds(i, 1)])
            self.go(2, other_x, (self.own.at[1 - x_at, self.p, at], self.last))

        def back_far(self):
            self.arrive()
            self.finish(other_x)

        def back_near(self):
            self.share(4, far_z, *[self.red.at[i, self.p, 2 * low + high] for i in range(2)])

        def back_x(self):
            self.share(5, near_z, *[self.red.at[i, self.p, pl.ds(2 * low, 2)] for i in range(2)])

    pieces_made = []

    def spread_dproj(part, cols):
        return [
            go(dproj.at[:, cols], dp_in.at[i, :, cols], s_p.at[part, i], r_p.at[part, i], group[i][0])
            for i in range(2)
        ]

    dp_got = [spread_dproj(0, pl.ds(0, DI))]
    for copy in n2_got:
        copy.wait_recv()
    d_all = [d_own] + [d_in.at[i] for i in range(3)]
    n2_all = [n2t[me]] + [n2_in[i] for i in range(3)]
    for p in range(2):
        value = total_of(n2_all, d_all, slice(OUT_W * p, OUT_W * p + OUT_W)).astype(BF)
        own_out[:, p] = value.reshape(2, 4, PR, OUT_W)
    steps = [
        kind(own_out, red_out, p, half_out, quart_out, last_out)
        for p, kind in enumerate((XFirst, ZFirst))
    ]
    for piece in steps:
        piece.over_x()
    rest = jnp.zeros((T - HEADS, T), F32)
    dstep = jnp.concatenate(dstep_rows + [rest], axis=0).T
    dlog = dlog + jnp.concatenate(dlog_rows + [rest], axis=0).T
    di16 = dinter.astype(BF)
    dact[:, DI:DI + STATE] = dot_tn(di16, out_state)
    dact[:, DI + STATE:] = dot(di16, in_state)
    upper = (row <= lane).astype(F32)
    ddecay = jnp.dot(upper, dlog, precision=lax.Precision.HIGHEST, preferred_element_type=F32)
    dstep = dstep + ddecay * rate
    draw = dstep * jax.nn.sigmoid(step_in)
    gs[5:6, 768:896] = colsum(draw)
    gs[5:6, 896:1024] = colsum(ddecay * step * rate)
    gs[5:6, 1024:1152] = dskip
    dproj[:, MAIN:] = draw.astype(BF)
    W = 256
    for k in range(0, CHAN, W):
        cols = slice(k, k + W)
        v, raw = conv[:, cols], ci[:, cols]
        sig = jax.nn.sigmoid(v)
        dconv = dact[:, cols] * (sig * (1.0 + v * (1.0 - sig)))
        gs[4:5, cols] = colsum(dconv)
        gs[KCONV - 1:KCONV, cols] = colsum(dconv * raw)
        dci = dconv * taps_ref[KCONV - 1:KCONV, cols]
        for j in range(1, KCONV):
            here = dconv * within[j]
            gs[KCONV - 1 - j:KCONV - j, cols] = colsum(here * pltpu.roll(raw, j, 0))
            dci = dci + pltpu.roll(here * taps_ref[KCONV - 1 - j:KCONV - j, cols], T - j, 0)
        dproj[:, DI + k:DI + k + W] = dci.astype(BF)

    dp_got.append(spread_dproj(1, pl.ds(DI, PADC - DI)))
    dn = dot_nt(dproj[:, MAIN:], tail[...])
    for k in range(0, MAIN, 256):
        dn = dn + dot_nt(dproj[:, k:k + 256], wi_ref[:, k:k + 256])
    xr = x * r1
    gs[5:6, 0:D] = colsum(dn * xr)
    u = dn * pg_ref[...]
    dx = r1 * (u - xr * jnp.mean(u * xr, axis=1, keepdims=True)) + dy
    gx_ref[...] = dx.astype(BF)

    small_copy = go(gs, srecv.at[0], s_s.at[0], r_s.at[0], core)
    for piece in steps:
        piece.near()
    forwarded = []
    for part, cols in enumerate((pl.ds(0, DI), pl.ds(DI, PADC - DI))):
        dp_got[part][1].wait_recv()
        forwarded.append(go(
            dp_in.at[1, :, cols], dp_in.at[2, :, cols], s_p.at[part, 2], r_p.at[part, 2], core
        ))
    for piece in steps:
        piece.far()
    for part in range(2):
        dp_got[part][0].wait_recv()
    for copy in n_got:
        copy.wait_recv()
    small_copy.wait_recv()
    sbuf[0] = gs[...] + srecv[0]
    small_copy = go(sbuf.at[0], srecv.at[1], s_s.at[1], r_s.at[1], other_y)
    for piece in steps:
        piece.back_far()
    n_all = [nt[me]] + [n_in[i] for i in range(3)]
    dp_all = [dproj] + [dp_in.at[i] for i in range(3)]

    def put(k, first, value):
        wide = value.shape[1]
        own_in[:, :, k, :, first:first + wide] = value.astype(BF).reshape(2, 2, PR, wide)

    forwarded[0].wait_recv()
    put(0, 0, total_of(n_all, dp_all, slice(0, IN_W)))
    forwarded[1].wait_recv()
    for k in range(1, 3):
        put(k, 0, total_of(n_all, dp_all, slice(IN_W * k, IN_W * k + IN_W)))
    put(3, 0, total_of(n_all, dp_all, slice(IN_W * 3, PADC)))
    put(3, PADC - 3 * IN_W, jnp.zeros((192, 4 * IN_W - PADC), F32))
    main = [
        kind(own_in, red_in, p, half_in, quart_in, last_in)
        for p, kind in enumerate((XFirst, ZFirst))
    ]
    for piece in main:
        piece.over_x()
    for piece in steps:
        piece.back_near()
    out_got = []
    for i, (peer, shard) in enumerate(group):
        out_part[i] = dot_tn(n2_in[i], wo_own[...]).astype(BF)
        out_got.append(go(out_part.at[i], out_in.at[i], s_o.at[i], r_o.at[i], peer))
    for s, (peer, piece_step) in enumerate(((other_x, "near"), (near_z, "far"), (far_z, "back_far"))):
        for piece in main:
            getattr(piece, piece_step)()
        small_copy.wait_recv()
        sbuf[s + 1] = sbuf[s] + srecv[s + 1]
        small_copy = go(sbuf.at[s + 1], srecv.at[s + 2], s_s.at[s + 2], r_s.at[s + 2], peer)
    for piece in steps:
        piece.back_x()
    for piece in main:
        piece.back_near()
    out = x_ref[...].astype(F32) + dot_tn(n2t[me], wo_own[...])
    for i in range(3):
        out_got[i].wait_recv()
        out = out + out_in[i].astype(F32)
    out_ref[...] = out.astype(BF)
    for piece in main:
        piece.back_x()
    small_copy.wait_recv()
    sm_out[...] = sbuf[3] + srecv[4]
    for piece in steps + main:
        piece.arrive()
    for copy in started:
        copy.wait_send()


def layer(tokens, cotangent, lens, w_in, w_out, params):
    vmem = pl.BlockSpec(memory_space=pltpu.VMEM)
    shape = jax.ShapeDtypeStruct
    dma = pltpu.SemaphoreType.DMA
    return pl.pallas_call(
        layer_kernel,
        out_shape=(
            shape((T, D), BF), shape((T, D), BF), shape((2, 2, 4, PR, OUT_W), BF),
            shape((2, 2, 4, PR, IN_W), BF), shape((8, CHAN), F32),
        ),
        in_specs=[vmem, vmem, pl.BlockSpec(memory_space=pltpu.SMEM)] + [vmem] * 3,
        out_specs=[vmem] * 5,
        scratch_shapes=[
            pltpu.VMEM((T, DI), F32), pltpu.VMEM((T, CHAN), F32), pltpu.VMEM((T, CHAN), F32),
            pltpu.VMEM((T, CHAN), BF), pltpu.VMEM((T, DI), F32), pltpu.VMEM((HEADS, T, T), F32),
            pltpu.VMEM((T, PADC), BF), pltpu.VMEM((D, 128), BF), pltpu.VMEM((4, 192, T), BF),
            pltpu.VMEM((4, 384, T), BF), pltpu.VMEM((T, DI), F32), pltpu.VMEM((T, D), BF),
            pltpu.VMEM((T, CHAN), F32),
            pltpu.VMEM((4, T, 384), BF), pltpu.VMEM((3, T, 384), BF), pltpu.VMEM((3, T, D), BF),
            pltpu.VMEM((3, T, D), BF), pltpu.VMEM((T, D), BF), pltpu.VMEM((3, T, D), BF),
            pltpu.VMEM((3, 192, T), BF), pltpu.VMEM((3, 384, T), BF), pltpu.VMEM((3, T, PADC), BF),
            pltpu.VMEM((2, 2, 4, PR, OUT_W), BF), pltpu.VMEM((2, 4, PR, OUT_W), BF),
            pltpu.VMEM((2, 2, PR, OUT_W), BF), pltpu.VMEM((2, PR, OUT_W), BF),
            pltpu.VMEM((2, 2, 4, PR, IN_W), BF), pltpu.VMEM((2, 4, PR, IN_W), BF),
            pltpu.VMEM((2, 2, PR, IN_W), BF), pltpu.VMEM((2, PR, IN_W), BF),
            pltpu.VMEM((8, CHAN), F32), pltpu.VMEM((4, 8, CHAN), F32), pltpu.VMEM((5, 8, CHAN), F32),
            dma((3,)), dma((3,)), dma((3,)), dma((3,)), dma((3,)), dma((3,)), dma((3,)), dma((3,)), dma((3,)), dma((3,)),
            dma((2, 3)), dma((2, 3)), dma((6, 4, 2)), dma((6, 4, 2)), dma((5,)), dma((5,)),
        ],
        compiler_params=pltpu.CompilerParams(
            collective_id=1, has_side_effects=True, vmem_limit_bytes=LAYER_BYTES
        ),
        name="layer",
    )(tokens, cotangent, lens, w_in, w_out, params)


def adamw_kernel(red_out, red_in, wi, mi, vi, wo, mo, vo, nwi, nmi, nvi, nwo, nmo, nvo):
    def update(cols, grad, refs, rate, part):
        at = (part, cols)
        gradient, master = grad.astype(F32), refs[0][at].astype(F32)
        first = beta_one * refs[1][at] + (1.0 - beta_one) * gradient
        second = beta_two * refs[2][at] + (1.0 - beta_two) * gradient * gradient
        root = jnp.sqrt(second * (1.0 / (1.0 - beta_two**STEP))) + adam_eps
        scale = rate / (1.0 - beta_one**STEP)
        new = (master * (1.0 - rate * 0.1) - scale * first / root, first, second)
        for ref, value in zip(refs[3:], new):
            ref[at] = value

    refs_in = (wi, mi, vi, nwi, nmi, nvi)
    refs_out = (wo, mo, vo, nwo, nmo, nvo)
    for k in range(4):
        wide = min(IN_W, CIN - IN_W * k)
        update(slice(IN_W * k, IN_W * k + wide), red_in[0, 0, k, :, :wide], refs_in, 0.05, slice(None))
    for p in range(2):
        for k in range(2):
            update(
                slice(OUT_W * p, OUT_W * p + OUT_W), red_out[0, p, k], refs_out, 0.04,
                slice(PR * k, PR * k + PR),
            )


def adamw_all(red_out, red_in, w_in, m_in, v_in, w_out, m_out, v_out):
    spec_in = pl.BlockSpec((PR, CIN), lambda i: (i, 0))
    spec_out = pl.BlockSpec((2 * PR, D), lambda i: (i, 0))
    return pl.pallas_call(
        adamw_kernel,
        grid=(4,),
        out_shape=[jax.ShapeDtypeStruct((192, CIN), F32)] * 3 + [jax.ShapeDtypeStruct((384, D), F32)] * 3,
        in_specs=[
            pl.BlockSpec((1, 2, 2, PR, OUT_W), lambda i: (i // 2, 0, i % 2, 0, 0)),
            pl.BlockSpec((1, 1, 4, PR, IN_W), lambda i: (i // 2, i % 2, 0, 0, 0)),
        ] + [spec_in] * 3 + [spec_out] * 3,
        out_specs=[spec_in] * 3 + [spec_out] * 3,
        compiler_params=pltpu.CompilerParams(vmem_limit_bytes=VMEM_BYTES),
        name="adamw",
    )(red_out, red_in, w_in, m_in, v_in, w_out, m_out, v_out)


def on_device_fast(
    tokens, cotangent, seq_lengths, w_in, w_out, w_small, m_in, v_in, m_out, v_out, m_small, v_small
):
    share = w_small.shape[0]
    small = jnp.pad(w_small, (0, 32 * 128 - share)).reshape(32, 128)
    full_in, full_small = gather_weights(w_in, small)
    packed = full_small.reshape(4, 32 * 128)[:, :share].reshape(4 * share).astype(F32)
    start = (KCONV + 1) * CHAN
    gains = start + 3 * HEADS
    heads = jnp.pad(packed[start:gains].reshape(3, HEADS), ((0, 0), (0, 128 - HEADS)))
    params = jnp.concatenate([
        packed[:start], packed[gains : gains + D], heads.reshape(-1), jnp.zeros(CHAN - D - 384, F32),
        packed[gains + D :], jnp.zeros(2 * CHAN - DI, F32),
    ]).reshape(8, CHAN)
    out, gx, red_out, red_in, sums = layer(
        tokens, cotangent, seq_lengths, full_in.reshape(D, CIN), w_out, params
    )
    flat = jnp.concatenate([
        sums[:5].reshape(-1), sums[5, D : D + HEADS], sums[5, D + 128 : D + 128 + HEADS],
        sums[5, D + 256 : D + 256 + HEADS], sums[5, :D], sums[6, :DI],
    ])
    share_small = lax.dynamic_slice_in_dim(flat, lax.axis_index("shard") * share, share)
    new = adamw_all(red_out, red_in, w_in, m_in, v_in, w_out, m_out, v_out)
    new_small = adamw(w_small, share_small, m_small, v_small, 0.3, 0.0)
    return (out, gx, *new, *new_small)


def solution(mesh):
    in_specs = (
        P(("replica", "shard"), None),
        P(("replica", "shard"), None),
        P(("replica", "shard"), None),
        P("shard", None),
        P("shard", None),
        P("shard"),
        P("shard", None),
        P("shard", None),
        P("shard", None),
        P("shard", None),
        P("shard"),
        P("shard"),
    )
    out_specs = (
        P(("replica", "shard"), None),
        P(("replica", "shard"), None),
        P("shard", None),
        P("shard", None),
        P("shard", None),
        P("shard", None),
        P("shard", None),
        P("shard", None),
        P("shard"),
        P("shard"),
        P("shard"),
    )
    fast = dict(mesh.shape) == {"replica": 8, "shard": 4}
    return jax.shard_map(
        on_device_fast if fast else on_device, mesh=mesh, in_specs=in_specs, out_specs=out_specs, check_vma=False
    )
```
